128 devices in a mesh: gx: 16 (over x_lo, y, core), gy: 8 (over z, x_hi).
Axes of the slice: x: 4 (x_hi: 2, x_lo: 2; x = x_hi * 2 + x_lo), y: 4, z: 4, core: 2. Of those that a mesh axis runs over, the one named last changes fastest.
Arguments:
- state: float32 [5, 64, 512, 1024], P(None, None, 'gx', 'gy'), may hold values from -6 to 6
- eddy: float32 [64, 512, 1024], P(None, 'gx', 'gy'), may hold values from 0.05 to 0.5
- shift_rows: int32 [64], replicated, may hold values from 0 to 511
- shift_cols: int32 [64], replicated, may hold values from 0 to 1023
- screen_of_level: int32 [64], replicated, may hold values from 0 to 31, as said below
Outputs:
- advanced: float32 [5, 64, 512, 1024], P(None, None, 'gx', 'gy')
- screens: float32 [32, 512, 1024], P('gy', 'gx')
The draws below stay inside these ranges and needn't reach their ends.
Inputs may be any that keep to these rules, and one draw needn't show every extreme that they name: `screen_of_level`: never falls from one level to the next; every screen receives 1 to 4 levels, and some screen exactly 4; the first 32 // 8 screens together receive at least 64 // 8 + 2 levels.
All inputs are finite; a program needn't handle non-finite values.
Results may differ from the reference program's by a relative error of at most 0.0003.
Values sent between devices are 32-bit elements; how exact they have to be, the bound alone decides.
No kernel may reach another device: no remote copies, remote signals or barrier semaphores. Data moves between devices by JAX's collectives and lax.ppermute only.
A program may use at most 256 MiB of HBM per device.

```python
import math
import jax
import jax.numpy as jnp
from jax import lax

NZ = 64
NS = 32
MOST_LEVELS = 4
NX = 512
NY = 1024
N_GY = 8


def draw_screen_of_level(key, part):
    key = jax.random.fold_in(key, 11)
    key_full, key_first, key_rest = jax.random.split(key, 3)
    per_screen = MOST_LEVELS - 1
    unit_total = NS * per_screen
    lead_screens = NS // N_GY
    needed = max(per_screen, NZ // N_GY + 2 - lead_screens)
    extra_total = NZ - NS
    unit_screen = jnp.repeat(jnp.arange(NS, dtype=jnp.int32), per_screen)
    full_screen = jax.random.randint(key_full, (), 0, lead_screens, dtype=jnp.int32)
    first_perm = jax.random.permutation(key_first, unit_total).astype(jnp.int32)
    in_lead = unit_screen < lead_screens
    lead_score = jnp.where(in_lead, first_perm - jnp.where(unit_screen == full_screen, unit_total, 0), 2 * unit_total + first_perm)
    lead_rank = jnp.argsort(jnp.argsort(lead_score, stable=True), stable=True)
    forced = lead_rank < needed
    rest_perm = jax.random.permutation(key_rest, unit_total).astype(jnp.int32)
    rest_score = jnp.where(forced, rest_perm - unit_total, rest_perm)
    rest_rank = jnp.argsort(jnp.argsort(rest_score, stable=True), stable=True)
    chosen = (rest_rank < extra_total).astype(jnp.int32)
    counts = 1 + jnp.sum(chosen.reshape(NS, per_screen), axis=1)
    ends = jnp.cumsum(counts)
    levels = jnp.arange(NZ, dtype=jnp.int32)
    return jnp.sum((ends[None, :] <= levels[:, None]).astype(jnp.int32), axis=1).astype(jnp.int32)


def set_ends(values, rng, smallest, top_value):
    longest = values.shape.index(max(values.shape))
    spots = []
    for shift in (0, 1):
        where = [jax.random.randint(jax.random.fold_in(rng, axis), (), 0, length) for axis, length in enumerate(values.shape)]
        where[longest] = (where[longest] + shift) % values.shape[longest]
        spots.append(tuple(where))
    return values.at[spots[0]].set(smallest).at[spots[1]].set(top_value)


def shard_levels(rng, dims, cuts, low, high):
    gain = 1.0
    for position, blocks in cuts:
        heights = jax.random.uniform(jax.random.fold_in(jax.random.fold_in(rng, 6), position), (blocks,), jnp.float32, low / len(cuts), high / len(cuts))
        gain = gain * jnp.repeat(jnp.exp(heights), dims[position] // blocks).reshape((-1,) + (1,) * (len(dims) - 1 - position))
    return gain


def scatter_about(own_key, dims, deviation, bound, cuts=(), held_as=jnp.bfloat16):
    values = jax.random.normal(own_key, dims, jnp.float32) * deviation
    if len(cuts) > 0:
        values = shard_levels(own_key, dims, cuts, -0.22, 0.18) * values
    return jnp.clip(values, min=-bound, max=bound).astype(held_as)


def setup_inputs(seed: int = 0) -> dict:
    key_list = jax.random.split(jax.random.key(seed), 6)
    state = scatter_about(key_list[0], (5, NZ, NX, NY), 1.0, 6.0, ((2, 16), (3, 8)), jnp.float32)
    eddy = jnp.clip(jnp.exp(math.log(0.5) - 2.3025851 * jax.random.uniform(key_list[1], (NZ, NX, NY), jnp.float32) ** shard_levels(key_list[1], (NZ, NX, NY), ((1, 16), (2, 8)), -0.2, 0.2)), 0.05, 0.5)
    shift_rows = set_ends(jax.random.randint(key_list[2], (NZ,), 0, NX), jax.random.fold_in(key_list[2], 1), 0, NX - 1).astype(jnp.int32)
    shift_cols = set_ends(jax.random.randint(key_list[3], (NZ,), 0, NY), jax.random.fold_in(key_list[3], 1), 0, NY - 1).astype(jnp.int32)
    screen_of_level = draw_screen_of_level(jax.random.fold_in(key_list[5], 71), 0)
    return {"state": state, "eddy": eddy, "shift_rows": shift_rows, "shift_cols": shift_cols, "screen_of_level": screen_of_level}


time_step = 0.1
buoyancy_gain = 0.3
heat_weight = -0.79
moist_weight = 0.56


def stencil(padded, dimension, length):
    def window(offset):
        return lax.slice_in_dim(padded, 3 + offset, 3 + offset + length, axis=dimension)

    centre = window(0)
    minus_one, minus_two, minus_three = window(-1), window(-2), window(-3)
    plus_one, plus_two, plus_three = window(1), window(2), window(3)
    central = (plus_three - minus_three) - 9.0 * (plus_two - minus_two) + 45.0 * (plus_one - minus_one)
    spread = (plus_three + minus_three) - 6.0 * (plus_two + minus_two) + 15.0 * (plus_one + minus_one) - 20.0 * centre
    laplace = plus_one + minus_one - 2.0 * centre
    return central, spread, laplace


def tendency(vertical_pad, east_pad, north_pad, velocity, eddy):
    east_wind, north_wind, upward = velocity
    z_central, z_spread, z_laplace = stencil(vertical_pad, 0, eddy.shape[0])
    x_central, x_spread, x_laplace = stencil(east_pad, 1, eddy.shape[1])
    y_central, y_spread, y_laplace = stencil(north_pad, 2, eddy.shape[2])
    transport = (east_wind * x_central - jnp.abs(east_wind) * x_spread
                 + north_wind * y_central - jnp.abs(north_wind) * y_spread
                 + upward * z_central - jnp.abs(upward) * z_spread) / 60.0
    return eddy * (x_laplace + y_laplace + z_laplace) - transport


def wrap_shift(layer, amount, dimension):
    length = layer.shape[dimension]
    doubled = jnp.concatenate([layer, layer], axis=dimension)
    first_row = ((length - amount) % length).astype(jnp.int32)
    return lax.dynamic_slice_in_dim(doubled, first_row, length, axis=dimension)


def displace_level(layer, row_amount, col_amount):
    return wrap_shift(wrap_shift(layer, row_amount, 0), col_amount, 1)


def reference(state, eddy, shift_rows, shift_cols, screen_of_level):
    velocity = (state[0], state[1], state[2])
    results = []
    for member in range(5):
        scalar_field = state[member]
        vertical_pad = jnp.pad(scalar_field, ((3, 3), (0, 0), (0, 0)), mode="edge")
        east_pad = jnp.pad(scalar_field, ((0, 0), (3, 3), (0, 0)), mode="wrap")
        north_pad = jnp.pad(scalar_field, ((0, 0), (0, 0), (3, 3)), mode="wrap")
        growth = tendency(vertical_pad, east_pad, north_pad, velocity, eddy)
        if member == 2:
            growth = growth + buoyancy_gain * state[3]
        results.append(scalar_field + time_step * growth)
    advanced = jnp.stack(results)
    refraction = heat_weight * advanced[3] + moist_weight * advanced[4]
    displaced = jax.vmap(displace_level)(refraction, shift_rows, shift_cols)
    one_hot = (screen_of_level[None, :] == jnp.arange(NS, dtype=jnp.int32)[:, None]).astype(jnp.float32)
    screens = jnp.einsum("sk,kij->sij", one_hot, displaced, precision=lax.Precision.HIGHEST)
    return advanced, screens
```

```python
import functools

import jax
import jax.numpy as jnp
import ml_dtypes
import numpy as np
from jax import lax
from jax.experimental import pallas as pl
from jax.experimental.pallas import tpu as pltpu
from jax.sharding import PartitionSpec as P

NS = 32

time_step = 0.1
buoyancy_gain = 0.3
heat_weight = -0.79
moist_weight = 0.56

LANES = 128
GROUP = 32
VMEM_LIMIT = 56 * 1024 * 1024
WHOLE = pl.BlockSpec(memory_space=pltpu.VMEM)
SCALARS = pl.BlockSpec(memory_space=pltpu.SMEM)
ANYWHERE = pl.BlockSpec(memory_space=pl.ANY)


def params():
    return pltpu.CompilerParams(vmem_limit_bytes=VMEM_LIMIT)


def f32(shape):
    return jax.ShapeDtypeStruct(shape, jnp.float32)


def pack_edges(value, count, rows, outs):
    top, bottom, low, high = outs
    lane = lax.broadcasted_iota(jnp.int32, (rows, LANES), 1)
    low_acc = jnp.zeros((rows, LANES), jnp.float32)
    high_acc = low_acc
    for level in range(count):
        tile = value(level)
        top[3 * level : 3 * level + 3] = tile[0:3]
        bottom[3 * level : 3 * level + 3] = tile[rows - 3 : rows]
        turned = pltpu.roll(tile, 3 * level, 1)
        place = lane - 3 * level
        low_acc = jnp.where((place >= 0) & (place < 3), turned, low_acc)
        high_acc = jnp.where(((place >= -3) & (place < 0)) | (place >= 125), turned, high_acc)
    low[0] = low_acc
    high[0] = high_acc


def q_edges_kernel(heat, moist, q, *outs):
    rows = q.shape[1]

    def value(level):
        tile = heat_weight * heat[0, level] + moist_weight * moist[0, level]
        q[level] = tile
        return tile

    pack_edges(value, q.shape[0], rows, outs)


def state_edges_kernel(after, state, *outs):
    pack_edges(lambda level: state[0, level], state.shape[1], state.shape[2], outs)


def edge_outputs(fields, levels, rows):
    groups = levels // GROUP
    shapes = [f32((fields * levels * 3, LANES))] * 2 + [f32((fields * groups, rows, LANES))] * 2
    return shapes, groups


def q_edges(state):
    levels, rows = state.shape[1:3]
    shapes, groups = edge_outputs(1, levels, rows)
    member = lambda n: pl.BlockSpec((1, GROUP, rows, LANES), lambda i: (n, i, 0, 0))
    return pl.pallas_call(
        q_edges_kernel,
        grid=(groups,),
        in_specs=[member(3), member(4)],
        out_specs=[pl.BlockSpec((GROUP, rows, LANES), lambda i: (i, 0, 0))]
        + [pl.BlockSpec((3 * GROUP, LANES), lambda i: (i, 0))] * 2
        + [pl.BlockSpec((1, rows, LANES), lambda i: (i, 0, 0))] * 2,
        out_shape=[f32((levels, rows, LANES))] + shapes,
        compiler_params=params(),
        name="q_edges",
    )(state, state)


def state_edges(state, after):
    fields, levels, rows = state.shape[:3]
    shapes, groups = edge_outputs(fields, levels, rows)
    return pl.pallas_call(
        state_edges_kernel,
        grid=(fields, groups),
        in_specs=[ANYWHERE, pl.BlockSpec((1, GROUP, rows, LANES), lambda m, i: (m, i, 0, 0))],
        out_specs=[pl.BlockSpec((3 * GROUP, LANES), lambda m, i: (m * groups + i, 0))] * 2
        + [pl.BlockSpec((1, rows, LANES), lambda m, i: (m * groups + i, 0, 0))] * 2,
        out_shape=shapes,
        compiler_params=params(),
        name="state_edges",
    )(after, state)


def ring(axis, step):
    count = lax.axis_size(axis)
    return [(i, (i + step) % count) for i in range(count)]


def exchange(edges):
    top, bottom, low, high = edges
    above = lax.ppermute(bottom, "gx", ring("gx", 1))
    below = lax.ppermute(top, "gx", ring("gx", -1))
    left = lax.ppermute(high, "gy", ring("gy", 1))
    right = lax.ppermute(low, "gy", ring("gy", -1))
    return above, below, left, right


def factors(wind, eddy):
    scale = time_step / 60.0
    winds = [wind(n) * scale for n in range(3)]
    sizes = [jnp.abs(w) for w in winds]
    mix = time_step * eddy
    keep = 1.0 - 6.0 * mix - 20.0 * (sizes[0] + sizes[1] + sizes[2])
    return winds, sizes, mix, keep


def along(near, wind, size):
    m3, m2, m1, p1, p2, p3 = near
    first = p1 + m1
    central = (p3 - m3) - 9.0 * (p2 - m2) + 45.0 * (p1 - m1)
    spread = (p3 + m3) - 6.0 * (p2 + m2) + 15.0 * first
    return first, size * spread - wind * central


SIDES = (-3, -2, -1, 1, 2, 3)
ROWS = 8


def fill_pad(tile, row_at, above, below, pad):
    rows = tile.shape[0]
    pad[8 : 8 + rows] = tile
    pad[5:8] = above[pl.ds(row_at, 3), :]
    pad[8 + rows : 11 + rows] = below[pl.ds(row_at, 3), :]


def step_rows(field, level, levels, at, group, back, left, right, pad, coefficients):
    winds, sizes, mix, keep = coefficients
    tile = field(level)
    east = [pad[8 + at + n : 8 + at + n + ROWS] for n in SIDES]
    lane = lax.broadcasted_iota(jnp.int32, (ROWS, LANES), 1)
    low, high = left[group, at : at + ROWS], right[group, at : at + ROWS]
    edge = jnp.where(lane < 64, pltpu.roll(high, back, 1), pltpu.roll(low, back, 1))
    north = [pltpu.roll(jnp.where(lane >= LANES - n, edge, tile), n, 1) for n in (3, 2, 1)]
    north += [pltpu.roll(jnp.where(lane < n, edge, tile), LANES - n, 1) for n in (1, 2, 3)]
    upward = [field(jnp.clip(level + n, 0, levels - 1)) for n in SIDES]
    total, result = 0.0, tile * keep
    for near, wind, size in zip((east, north, upward), winds, sizes):
        first, moved = along(near, wind, size)
        total = total + first
        result = result + moved
    return result + mix * total


def lane_place(level):
    return level // GROUP, lax.rem(LANES - 3 * lax.rem(level, GROUP), LANES)


def lane_weights():
    inside = np.zeros((LANES, 3, LANES), np.float32)
    beyond = np.zeros((LANES, 3, LANES), np.float32)
    for j in range(LANES):
        for n, terms in ((1, (1, 45, 15)), (2, (0, -9, -6)), (3, (0, 1, 1))):
            for sign in (1, -1):
                source = j + sign * n
                where = inside if 0 <= source < LANES else beyond
                for which in range(3):
                    factor = terms[which] * (sign if which == 1 else 1)
                    where[source % LANES, which, j] += factor
    inside, beyond = inside.reshape(LANES, -1), beyond.reshape(LANES, -1)
    return np.concatenate([inside, inside, beyond, beyond]).astype(ml_dtypes.bfloat16)


def halves(tile):
    high = tile.astype(jnp.bfloat16)
    return high, (tile - high.astype(jnp.float32)).astype(jnp.bfloat16)


PAIR = 4
CHUNK = 8


def advance_kernel(chunk, *refs):
    state, eddy, above, below, left, right, weights, after, out, pad, even, odd = refs
    fields, levels, rows = state.shape[:3]
    groups = levels // GROUP
    base = pl.program_id(0) * chunk
    lane = lax.broadcasted_iota(jnp.int32, (rows, LANES), 1)

    def multiply(start, product):
        parts = []
        for one in range(PAIR):
            level = jnp.minimum(start + one, levels - 1)
            group, back = lane_place(level)
            for member in range(fields):
                high = pltpu.roll(right[member * groups + group], back, 1)
                low = pltpu.roll(left[member * groups + group], back, 1)
                edge = jnp.where(lane < 3, high, jnp.where(lane >= LANES - 3, low, 0.0))
                parts.append(jnp.concatenate(halves(state[member, level]) + halves(edge), axis=1))
        product[...] = jnp.dot(
            jnp.concatenate(parts, axis=0), weights[...], preferred_element_type=jnp.float32
        )

    def finish(step, product):
        for one in range(PAIR):
            index = step * PAIR + one
            level = base + index
            for member in range(fields):
                fill_pad(state[member, level], 3 * (member * levels + level), above, below, pad.at[one, member])
            for at in range(0, rows, ROWS):
                here = slice(at, at + ROWS)
                winds, sizes, mix, keep = factors(lambda n: state[n, level, here], eddy[level, here])
                for member in range(fields):
                    tile = state[member, level, here]
                    east = [pad[one, member, 8 + at + n : 8 + at + n + ROWS] for n in SIDES]
                    upward = [state[member, jnp.clip(level + n, 0, levels - 1), here] for n in SIDES]
                    spot = (one * fields + member) * rows + at
                    spot = slice(spot, spot + ROWS)
                    total = product[spot, 0:LANES]
                    result = tile * keep + (
                        sizes[1] * product[spot, 2 * LANES : 3 * LANES]
                        - winds[1] * product[spot, LANES : 2 * LANES]
                    )
                    for near, axis in ((east, 0), (upward, 2)):
                        first, moved = along(near, winds[axis], sizes[axis])
                        total = total + first
                        result = result + moved
                    result = result + mix * total
                    if member == 2:
                        result = result + (time_step * buoyancy_gain) * state[3, level, here]
                    out[member, index, here] = result

    @pl.when(pl.program_id(0) == 0)
    def _():
        multiply(0, even)

    def body(twice, carry):
        step = 2 * twice
        multiply(base + (step + 1) * PAIR, odd)
        finish(step, even)
        multiply(base + (step + 2) * PAIR, even)
        finish(step + 1, odd)
        return carry

    lax.fori_loop(0, chunk // PAIR // 2, body, 0)


def advance(state, eddy, halos, after):
    fields, levels, rows = state.shape[:3]
    chunk = CHUNK
    return pl.pallas_call(
        functools.partial(advance_kernel, chunk),
        grid=(levels // chunk,),
        in_specs=[WHOLE] * 7 + [ANYWHERE],
        out_specs=pl.BlockSpec((fields, chunk, rows, LANES), lambda i: (0, i, 0, 0)),
        out_shape=f32(state.shape),
        scratch_shapes=[
            pltpu.VMEM((PAIR, fields, rows + 16, LANES), jnp.float32),
            pltpu.VMEM((PAIR * fields * rows, 3 * LANES), jnp.float32),
            pltpu.VMEM((PAIR * fields * rows, 3 * LANES), jnp.float32),
        ],
        compiler_params=params(),
        cost_estimate=pl.CostEstimate(
            flops=state.size * 60, bytes_accessed=state.size * 10, transcendentals=0
        ),
        name="advance",
    )(state, eddy, *halos, jnp.asarray(lane_weights()), after)


def row_places(shift_rows, filled, level, rows, devices):
    shift = shift_rows[level]
    block, rest = shift // rows, lax.rem(shift, rows)
    after = lax.rem(block + 1, devices)
    near = filled[block]
    filled[block] = near + rows - rest
    far = filled[after]
    filled[after] = far + rest
    return block, after, rest, near, far


UNROLL = 4


def send_rows_kernel(chunk, capacity, here, shift_rows, q, wind, eddy, *refs):
    above, below, left, right, out, packed, pad, double, filled, sem = refs
    levels, rows = q.shape[:2]
    devices = out.shape[0]
    stride = capacity + rows
    base = pl.program_id(0) * chunk

    @pl.when(pl.program_id(0) == 0)
    def _():
        for d in range(devices):
            filled[d] = 0

    def one(index, slot):
        level = base + index
        group, back = lane_place(level)
        ready = double.at[slot]
        fill_pad(q[level], 3 * level, above, below, pad.at[slot])
        for at in range(0, rows, ROWS):
            strip = slice(at, at + ROWS)
            coefficients = factors(lambda n: wind[n, index, strip], eddy[index, strip])
            ready[strip] = step_rows(
                lambda k: q[k, strip], level, levels, at, group, back, left, right, pad.at[slot], coefficients
            )

    def body(step, carry):
        for slot in range(UNROLL):
            one(step * UNROLL + slot, slot)
        for slot in range(UNROLL):
            ready = double.at[slot]
            level = base + step * UNROLL + slot
            block, after, rest, near, far = row_places(shift_rows, filled, level, rows, devices)
            packed[pl.ds(block * stride + near, rows), :] = ready[0:rows]
            packed[pl.ds(after * stride + far, rows), :] = ready[pl.ds(rows - rest, rows), :]
        return carry

    lax.fori_loop(0, chunk // UNROLL, body, 0)

    @pl.when(pl.program_id(0) == pl.num_programs(0) - 1)
    def _():
        copies = [
            pltpu.make_async_copy(
                packed.at[pl.ds(d * stride, capacity)], out.at[lax.rem(here[0] + d, devices)], sem.at[d]
            )
            for d in range(devices)
        ]
        for copy in copies:
            copy.start()
        for copy in copies:
            copy.wait()


def send_rows(capacity, devices, here, shift_rows, q, state, eddy, halos):
    levels, rows = q.shape[:2]
    chunk = 16
    return pl.pallas_call(
        functools.partial(send_rows_kernel, chunk, capacity),
        grid=(levels // chunk,),
        in_specs=[
            SCALARS,
            SCALARS,
            WHOLE,
            pl.BlockSpec((3, chunk, rows, LANES), lambda i: (0, i, 0, 0)),
            pl.BlockSpec((chunk, rows, LANES), lambda i: (i, 0, 0)),
        ]
        + [WHOLE] * 4,
        out_specs=ANYWHERE,
        out_shape=f32((devices, capacity, LANES)),
        scratch_shapes=[
            pltpu.VMEM((devices * (capacity + rows), LANES), jnp.float32),
            pltpu.VMEM((UNROLL, rows + 16, LANES), jnp.float32),
            pltpu.VMEM((UNROLL, 2 * rows, LANES), jnp.float32),
            pltpu.SMEM((devices,), jnp.int32),
            pltpu.SemaphoreType.DMA((devices,)),
        ],
        compiler_params=params(),
        name="send_rows",
    )(here, shift_rows, q, state, eddy, *halos)


def place_rows_kernel(levels, here, shift_rows, got, out, held, filled, sem):
    devices, capacity = got.shape[:2]
    rows = out.shape[1]
    me = here[0]
    copies = [
        pltpu.make_async_copy(got.at[d], held.at[pl.ds(rows + d * capacity, capacity)], sem.at[d])
        for d in range(devices)
    ]
    for copy in copies:
        copy.start()
    for d in range(devices):
        filled[d] = 0
    for copy in copies:
        copy.wait()
    row = lax.broadcasted_iota(jnp.int32, (rows, LANES), 0)

    def body(level, carry):
        block, after, rest, near, far = row_places(shift_rows, filled, level, rows, devices)
        near_from = lax.rem(me - block + devices, devices)
        far_from = lax.rem(me - after + devices, devices)
        near_tile = held[pl.ds(rows + near_from * capacity + near - rest, rows), :]
        far_tile = held[pl.ds(rows + far_from * capacity + far, rows), :]
        out[level] = jnp.where(row < rest, far_tile, near_tile)
        return carry

    lax.fori_loop(0, levels, body, 0)


def place_rows(here, shift_rows, got, rows, spare):
    devices, capacity = got.shape[:2]
    levels = shift_rows.shape[0]
    return pl.pallas_call(
        functools.partial(place_rows_kernel, levels),
        in_specs=[SCALARS, SCALARS, ANYWHERE],
        out_specs=WHOLE,
        out_shape=f32((levels + spare, rows, LANES)),
        scratch_shapes=[
            pltpu.VMEM((devices * capacity + 2 * rows, LANES), jnp.float32),
            pltpu.SMEM((devices,), jnp.int32),
            pltpu.SemaphoreType.DMA((devices,)),
        ],
        compiler_params=params(),
        name="place_rows",
    )(here, shift_rows, got)


def pick_levels_kernel(starts, placed, out, sem):
    owners, capacity = out.shape[:2]
    copies = [
        pltpu.make_async_copy(placed.at[pl.ds(starts[g], capacity)], out.at[g], sem.at[g])
        for g in range(owners)
    ]
    for copy in copies:
        copy.start()
    for copy in copies:
        copy.wait()


def pick_levels(starts, placed, owners, capacity):
    return pl.pallas_call(
        pick_levels_kernel,
        in_specs=[SCALARS, ANYWHERE],
        out_specs=ANYWHERE,
        out_shape=f32((owners, capacity) + placed.shape[1:]),
        scratch_shapes=[pltpu.SemaphoreType.DMA((owners,))],
        compiler_params=params(),
        name="pick_levels",
    )(starts, placed)


def sum_screens_kernel(here, starts, shift_cols, screen_of_level, got, out):
    owners = got.shape[0]
    screens, rows = out.shape[:2]
    me = here[1]
    first = starts[me]
    lane = lax.broadcasted_iota(jnp.int32, (rows, LANES), 1)
    out[...] = jnp.zeros(out.shape, jnp.float32)

    def body(index, carry):
        level = first + index
        shift = shift_cols[level]
        block, rest = shift // LANES, lax.rem(shift, LANES)
        screen = screen_of_level[level] - me * screens
        for t in range(owners):
            near = got[lax.rem(t - block + owners, owners), index]
            far = got[lax.rem(t - block - 1 + owners, owners), index]
            both = pltpu.roll(jnp.where(lane < LANES - rest, near, far), rest, 1)
            out[screen, :, t * LANES : (t + 1) * LANES] += both
        return carry

    lax.fori_loop(0, starts[me + 1] - first, body, 0)


def sum_screens(here, starts, shift_cols, screen_of_level, got, screens):
    owners, _, rows = got.shape[:3]
    return pl.pallas_call(
        sum_screens_kernel,
        in_specs=[SCALARS] * 4 + [WHOLE],
        out_specs=WHOLE,
        out_shape=f32((screens, rows, owners * LANES)),
        compiler_params=params(),
        name="sum_screens",
    )(here, starts, shift_cols, screen_of_level, got)


def swap(block, axis):
    return lax.all_to_all(block, axis, split_axis=0, concat_axis=0, tiled=True)


ROW_CAPACITIES = (192, 208, 224, 240, 256, 288, 320, 384)
LEVEL_CAPACITIES = (10, 11, 12, 13, 14)


def smallest(sizes, need):
    return jnp.sum((need > jnp.array(sizes, jnp.int32)).astype(jnp.int32))


def local(state, eddy, shift_rows, shift_cols, screen_of_level):
    levels, rows = state.shape[1:3]
    devices, owners = lax.axis_size("gx"), lax.axis_size("gy")
    per_owner = NS // owners
    most = 4 * per_owner
    here = jnp.stack([lax.axis_index("gx"), lax.axis_index("gy")]).astype(jnp.int32)

    block, rest = shift_rows // rows, shift_rows % rows
    place = jnp.arange(devices, dtype=jnp.int32)[:, None]
    rows_sent = jnp.sum(
        jnp.where(place == block[None], rows - rest[None], 0)
        + jnp.where(place == (block[None] + 1) % devices, rest[None], 0),
        axis=1,
    )
    bounds = per_owner * jnp.arange(owners + 1, dtype=jnp.int32)[:, None]
    starts = jnp.sum((screen_of_level[None] < bounds).astype(jnp.int32), axis=1)
    row_choice = smallest(ROW_CAPACITIES, jnp.max(rows_sent))
    level_choice = smallest(LEVEL_CAPACITIES, jnp.max(starts[1:] - starts[:-1]))

    q, *edges = q_edges(state)
    q_halos = exchange(edges)

    def move_rows(capacity):
        def branch(here, state, eddy, shift_rows, q, *q_halos):
            out = send_rows(capacity, devices, here, shift_rows, q, state, eddy, q_halos)
            got = swap(out, "gx")
            halos = exchange(state_edges(state, out))
            return place_rows(here, shift_rows, got, rows, most), *halos

        return branch

    placed, *halos = lax.switch(
        row_choice,
        [move_rows(c) for c in ROW_CAPACITIES + (levels * rows,)],
        here, state, eddy, shift_rows, q, *q_halos,
    )

    def to_screens(capacity):
        def branch(here, starts, shift_cols, screen_of_level, placed, state, eddy, *halos):
            out = pick_levels(starts, placed, owners, capacity)
            got = swap(out, "gy")
            advanced = advance(state, eddy, halos, out)
            return advanced, sum_screens(here, starts, shift_cols, screen_of_level, got, per_owner)

        return branch

    return lax.switch(
        level_choice,
        [to_screens(c) for c in LEVEL_CAPACITIES + (most,)],
        here, starts, shift_cols, screen_of_level, placed, state, eddy, *halos,
    )


def solution(mesh):
    placed = (P(None, None, "gx", "gy"), P(None, "gx", "gy"), P(), P(), P())
    return jax.shard_map(
        local,
        mesh=mesh,
        in_specs=placed,
        out_specs=(P(None, None, "gx", "gy"), P("gy", "gx", None)),
        check_vma=False,
    )
```

```python
import functools

import jax
import jax.numpy as jnp
import ml_dtypes
import numpy as np
from jax import lax
from jax.experimental import pallas as pl
from jax.experimental.pallas import tpu as pltpu
from jax.sharding import PartitionSpec as P

NS = 32

time_step = 0.1
buoyancy_gain = 0.3
heat_weight = -0.79
moist_weight = 0.56

LANES = 128
GROUP = 32
WHOLE = pl.BlockSpec(memory_space=pltpu.VMEM)
SCALARS = pl.BlockSpec(memory_space=pltpu.SMEM)
ANYWHERE = pl.BlockSpec(memory_space=pl.ANY)


def params(mebibytes):
    return pltpu.CompilerParams(vmem_limit_bytes=mebibytes * 1024 * 1024)


def f32(shape):
    return jax.ShapeDtypeStruct(shape, jnp.float32)


def pack_edges(value, count, rows, outs):
    top, bottom, low, high = outs
    lane = lax.broadcasted_iota(jnp.int32, (rows, LANES), 1)
    low_acc = jnp.zeros((rows, LANES), jnp.float32)
    high_acc = low_acc
    for level in range(count):
        tile = value(level)
        top[3 * level : 3 * level + 3] = tile[0:3]
        bottom[3 * level : 3 * level + 3] = tile[rows - 3 : rows]
        turned = pltpu.roll(tile, 3 * level, 1)
        place = lane - 3 * level
        low_acc = jnp.where((place >= 0) & (place < 3), turned, low_acc)
        high_acc = jnp.where(((place >= -3) & (place < 0)) | (place >= 125), turned, high_acc)
    low[0] = low_acc
    high[0] = high_acc


def q_edges_kernel(heat, moist, q, *outs):
    rows = q.shape[1]

    def value(level):
        tile = heat_weight * heat[0, level] + moist_weight * moist[0, level]
        q[level] = tile
        return tile

    pack_edges(value, q.shape[0], rows, outs)


def state_edges_kernel(after, state, top, bottom, low, high):
    levels, rows = state.shape[1:3]
    for group in range(levels // GROUP):
        first = group * GROUP
        strip = pl.ds(3 * first, 3 * GROUP)
        one = pl.ds(group, 1)
        outs = (top.at[strip], bottom.at[strip], low.at[one], high.at[one])
        pack_edges(lambda level: state[0, first + level], GROUP, rows, outs)


def edge_outputs(fields, levels, rows):
    groups = levels // GROUP
    shapes = [f32((fields * levels * 3, LANES))] * 2 + [f32((fields * groups, rows, LANES))] * 2
    return shapes, groups


def q_edges(state):
    levels, rows = state.shape[1:3]
    shapes, groups = edge_outputs(1, levels, rows)
    member = lambda n: pl.BlockSpec((1, GROUP, rows, LANES), lambda i: (n, i, 0, 0))
    return pl.pallas_call(
        q_edges_kernel,
        grid=(groups,),
        in_specs=[member(3), member(4)],
        out_specs=[pl.BlockSpec((GROUP, rows, LANES), lambda i: (i, 0, 0))]
        + [pl.BlockSpec((3 * GROUP, LANES), lambda i: (i, 0))] * 2
        + [pl.BlockSpec((1, rows, LANES), lambda i: (i, 0, 0))] * 2,
        out_shape=[f32((levels, rows, LANES))] + shapes,
        compiler_params=params(63),
        name="q_edges",
    )(state, state)


def state_edges(state, after):
    levels, rows = state.shape[1:3]
    fields = 4
    shapes, groups = edge_outputs(fields, levels, rows)
    return pl.pallas_call(
        state_edges_kernel,
        grid=(fields,),
        in_specs=[ANYWHERE, pl.BlockSpec((1, levels, rows, LANES), lambda m: (m, 0, 0, 0))],
        out_specs=[pl.BlockSpec((3 * levels, LANES), lambda m: (m, 0))] * 2
        + [pl.BlockSpec((groups, rows, LANES), lambda m: (m, 0, 0))] * 2,
        out_shape=shapes,
        compiler_params=params(63),
        cost_estimate=pl.CostEstimate(flops=0, bytes_accessed=60_000_000, transcendentals=0),
        name="state_edges",
    )(after, state)


def ring(axis, step):
    count = lax.axis_size(axis)
    return [(i, (i + step) % count) for i in range(count)]


def exchange(edges):
    top, bottom, low, high = edges
    left = lax.ppermute(high, "gy", ring("gy", 1))
    right = lax.ppermute(low, "gy", ring("gy", -1))
    above = lax.ppermute(bottom, "gx", ring("gx", 1))
    below = lax.ppermute(top, "gx", ring("gx", -1))
    return above, below, left, right


def factors(wind, eddy):
    scale = time_step / 60.0
    winds = [wind(n) * scale for n in range(3)]
    sizes = [jnp.abs(w) for w in winds]
    mix = time_step * eddy
    keep = 1.0 - 6.0 * mix - 20.0 * (sizes[0] + sizes[1] + sizes[2])
    return winds, sizes, mix, keep


def along(near, wind, size):
    m3, m2, m1, p1, p2, p3 = near
    first = p1 + m1
    central = (p3 - m3) - 9.0 * (p2 - m2) + 45.0 * (p1 - m1)
    spread = (p3 + m3) - 6.0 * (p2 + m2) + 15.0 * first
    return first, size * spread - wind * central


SIDES = (-3, -2, -1, 1, 2, 3)
ROWS = 8


def fill_pad(tile, row_at, above, below, pad):
    rows = tile.shape[0]
    pad[8 : 8 + rows] = tile
    pad[5:8] = above[pl.ds(row_at, 3), :]
    pad[8 + rows : 11 + rows] = below[pl.ds(row_at, 3), :]


def step_rows(field, level, levels, at, group, back, left, right, pad, coefficients):
    winds, sizes, mix, keep = coefficients
    tile = field(level)
    east = [pad[8 + at + n : 8 + at + n + ROWS] for n in SIDES]
    lane = lax.broadcasted_iota(jnp.int32, (ROWS, LANES), 1)
    low, high = left[group, at : at + ROWS], right[group, at : at + ROWS]
    edge = jnp.where(lane < 64, pltpu.roll(high, back, 1), pltpu.roll(low, back, 1))
    north = [pltpu.roll(jnp.where(lane >= LANES - n, edge, tile), n, 1) for n in (3, 2, 1)]
    north += [pltpu.roll(jnp.where(lane < n, edge, tile), LANES - n, 1) for n in (1, 2, 3)]
    upward = [field(jnp.clip(level + n, 0, levels - 1)) for n in SIDES]
    total, result = 0.0, tile * keep
    for near, wind, size in zip((east, north, upward), winds, sizes):
        first, moved = along(near, wind, size)
        total = total + first
        result = result + moved
    return result + mix * total


def lane_place(level):
    return level // GROUP, lax.rem(LANES - 3 * lax.rem(level, GROUP), LANES)


def lane_weights():
    inside = np.zeros((LANES, 3, LANES), np.float32)
    beyond = np.zeros((LANES, 3, LANES), np.float32)
    for j in range(LANES):
        for n, terms in ((1, (1, 45, 15)), (2, (0, -9, -6)), (3, (0, 1, 1))):
            for sign in (1, -1):
                source = j + sign * n
                where = inside if 0 <= source < LANES else beyond
                for which in range(3):
                    factor = terms[which] * (sign if which == 1 else 1)
                    where[source % LANES, which, j] += factor
    inside, beyond = inside.reshape(LANES, -1), beyond.reshape(LANES, -1)
    return np.concatenate([inside, inside, beyond, beyond]).astype(ml_dtypes.bfloat16)


def halves(tile):
    high = tile.astype(jnp.bfloat16)
    return high, (tile - high.astype(jnp.float32)).astype(jnp.bfloat16)


PAIR = 4
CHUNK = 8


def advance_kernel(chunk, *refs):
    state, eddy, above, below, left, right, *others, weights, after, out, pad, even, odd = refs[:-4]
    moist = refs[-4:]
    fields, levels, rows = state.shape[:3]
    groups = levels // GROUP
    base = pl.program_id(0) * chunk
    lane = lax.broadcasted_iota(jnp.int32, (rows, LANES), 1)

    def multiply(start, product):
        parts = []
        for one in range(PAIR):
            level = jnp.minimum(start + one, levels - 1)
            group, back = lane_place(level)
            for member in range(fields):
                last = member == fields - 1
                at = group if last else member * groups + group
                high = pltpu.roll((moist[3] if last else right)[at], back, 1)
                low = pltpu.roll((moist[2] if last else left)[at], back, 1)
                edge = jnp.where(lane < 3, high, jnp.where(lane >= LANES - 3, low, 0.0))
                parts.append(jnp.concatenate(halves(state[member, level]) + halves(edge), axis=1))
        product[...] = jnp.dot(
            jnp.concatenate(parts, axis=0), weights[...], preferred_element_type=jnp.float32
        )

    def finish(step, product):
        for one in range(PAIR):
            index = step * PAIR + one
            level = base + index
            for member in range(fields):
                last = member == fields - 1
                fill_pad(
                    state[member, level],
                    3 * level if last else 3 * (member * levels + level),
                    moist[0] if last else above,
                    moist[1] if last else below,
                    pad.at[one, member],
                )
            for at in range(0, rows, ROWS):
                here = slice(at, at + ROWS)
                winds, sizes, mix, keep = factors(lambda n: state[n, level, here], eddy[level, here])
                for member in range(fields):
                    tile = state[member, level, here]
                    east = [pad[one, member, 8 + at + n : 8 + at + n + ROWS] for n in SIDES]
                    upward = [state[member, jnp.clip(level + n, 0, levels - 1), here] for n in SIDES]
                    spot = (one * fields + member) * rows + at
                    spot = slice(spot, spot + ROWS)
                    total = product[spot, 0:LANES]
                    result = tile * keep + (
                        sizes[1] * product[spot, 2 * LANES : 3 * LANES]
                        - winds[1] * product[spot, LANES : 2 * LANES]
                    )
                    for near, axis in ((east, 0), (upward, 2)):
                        first, moved = along(near, winds[axis], sizes[axis])
                        total = total + first
                        result = result + moved
                    result = result + mix * total
                    if member == 2:
                        result = result + (time_step * buoyancy_gain) * state[3, level, here]
                    out[member, index, here] = result

    @pl.when(pl.program_id(0) == 0)
    def _():
        for mine, heat, both in zip(moist, (above, below, left, right), others):
            length = mine.shape[0]
            fourth = heat[pl.ds(3 * length, length)]
            mine[...] = (both[...] - heat_weight * fourth) * (1.0 / moist_weight)
        multiply(0, even)

    def body(twice, carry):
        step = 2 * twice
        multiply(base + (step + 1) * PAIR, odd)
        finish(step, even)
        multiply(base + (step + 2) * PAIR, even)
        finish(step + 1, odd)
        return carry

    lax.fori_loop(0, chunk // PAIR // 2, body, 0)


def advance(state, eddy, halos, q_halos, after):
    fields, levels, rows = state.shape[:3]
    chunk = CHUNK
    return pl.pallas_call(
        functools.partial(advance_kernel, chunk),
        grid=(levels // chunk,),
        in_specs=[WHOLE] * 11 + [ANYWHERE],
        out_specs=pl.BlockSpec((fields, chunk, rows, LANES), lambda i: (0, i, 0, 0)),
        out_shape=f32(state.shape),
        scratch_shapes=[
            pltpu.VMEM((PAIR, fields, rows + 16, LANES), jnp.float32),
            pltpu.VMEM((PAIR * fields * rows, 3 * LANES), jnp.float32),
            pltpu.VMEM((PAIR * fields * rows, 3 * LANES), jnp.float32),
        ]
        + [pltpu.VMEM(h.shape, jnp.float32) for h in q_halos],
        compiler_params=params(63),
        cost_estimate=pl.CostEstimate(
            flops=0, bytes_accessed=200_000_000, transcendentals=0
        ),
        name="advance",
    )(state, eddy, *halos, *q_halos, jnp.asarray(lane_weights()), after)


def row_places(shift_rows, filled, level, rows, devices):
    shift = shift_rows[level]
    block, rest = lax.div(shift, rows), lax.rem(shift, rows)
    after = lax.select(block == devices - 1, 0, block + 1)
    near = filled[block]
    filled[block] = near + rows - rest
    far = filled[after]
    filled[after] = far + rest
    return block, after, rest, near, far


UNROLL = 4


def send_rows_kernel(chunk, here, shift_rows, q, wind, eddy, *refs):
    above, below, left, right, out, over, packed, pad, double, filled, sems = refs
    levels, rows = q.shape[:2]
    devices, capacity = out.shape[:2]
    stride = capacity + over.shape[1] + rows
    base = pl.program_id(0) * chunk

    @pl.when(pl.program_id(0) == 0)
    def _():
        for d in range(devices):
            filled[d] = 0

    def one(index, slot):
        level = base + index
        group, back = lane_place(level)
        ready = double.at[slot]
        fill_pad(q[level], 3 * level, above, below, pad.at[slot])
        for at in range(0, rows, ROWS):
            strip = slice(at, at + ROWS)
            coefficients = factors(lambda n: wind[n, index, strip], eddy[index, strip])
            ready[strip] = step_rows(
                lambda k: q[k, strip], level, levels, at, group, back, left, right, pad.at[slot], coefficients
            )

    def body(step, carry):
        for slot in range(UNROLL):
            one(step * UNROLL + slot, slot)
        for slot in range(UNROLL):
            ready = double.at[slot]
            level = base + step * UNROLL + slot
            block, after, rest, near, far = row_places(shift_rows, filled, level, rows, devices)
            packed[pl.ds(block * stride + near, rows), :] = ready[0:rows]
            packed[pl.ds(after * stride + far, rows), :] = ready[pl.ds(rows - rest, rows), :]
        return carry

    lax.fori_loop(0, chunk // UNROLL, body, 0)

    @pl.when(pl.program_id(0) == pl.num_programs(0) - 1)
    def _():
        copies = [
            pltpu.make_async_copy(
                packed.at[pl.ds(d * stride, capacity)], out.at[lax.rem(here[0] + d, devices)], sems.at[0, d]
            )
            for d in range(devices)
        ]
        for copy in copies:
            copy.start()
        for copy in copies:
            copy.wait()
        for d in range(devices):

            @pl.when(filled[d] > capacity)
            def _():
                copy = pltpu.make_async_copy(
                    packed.at[pl.ds(d * stride + capacity, over.shape[1])],
                    over.at[lax.rem(here[0] + d, devices)],
                    sems.at[1, d],
                )
                copy.start()
                copy.wait()


def send_rows(capacity, beyond, devices, here, shift_rows, q, state, eddy, halos):
    levels, rows = q.shape[:2]
    chunk = 16
    return pl.pallas_call(
        functools.partial(send_rows_kernel, chunk),
        grid=(levels // chunk,),
        in_specs=[
            SCALARS,
            SCALARS,
            WHOLE,
            pl.BlockSpec((3, chunk, rows, LANES), lambda i: (0, i, 0, 0)),
            pl.BlockSpec((chunk, rows, LANES), lambda i: (i, 0, 0)),
        ]
        + [WHOLE] * 4,
        out_specs=[ANYWHERE] * 2,
        out_shape=[
            f32((devices, capacity, LANES)),
            f32((devices, beyond, LANES)),
        ],
        scratch_shapes=[
            pltpu.VMEM((devices * (capacity + beyond + rows), LANES), jnp.float32),
            pltpu.VMEM((UNROLL, rows + 16, LANES), jnp.float32),
            pltpu.VMEM((UNROLL, 2 * rows, LANES), jnp.float32),
            pltpu.SMEM((devices,), jnp.int32),
            pltpu.SemaphoreType.DMA((2, devices)),
        ],
        compiler_params=params(63),
        name="send_rows",
    )(here, shift_rows, q, state, eddy, *halos)


def place_rows_kernel(here, sent, shift_rows, starts, screen_of_level, got, over, out, extra, held, tiles, filled, sems):
    devices, capacity = got.shape[:2]
    owners, slots, rows = out.shape[:3]
    levels = shift_rows.shape[0]
    stride = capacity + over.shape[1]
    per_owner = NS // owners
    me = here[0]
    copies = [
        pltpu.make_async_copy(got.at[d], held.at[pl.ds(rows + d * stride, capacity)], sems.at[0, d])
        for d in range(devices)
    ]
    for copy in copies:
        copy.start()
    for d in range(devices):
        filled[d] = 0
    for copy in copies:
        copy.wait()
    for d in range(devices):

        @pl.when(sent[lax.rem(me - d + devices, devices)] > capacity)
        def _():
            copy = pltpu.make_async_copy(
                over.at[d], held.at[pl.ds(rows + d * stride + capacity, over.shape[1])], sems.at[1, d]
            )
            copy.start()
            copy.wait()

    row = lax.broadcasted_iota(jnp.int32, (rows, LANES), 0)

    def place(level, carry):
        block, after, rest, near, far = row_places(shift_rows, filled, level, rows, devices)
        near_from = lax.select(me >= block, me - block, me - block + devices)
        far_from = lax.select(me >= after, me - after, me - after + devices)
        near_tile = held[pl.ds(rows + near_from * stride + near - rest, rows), :]
        far_tile = held[pl.ds(rows + far_from * stride + far, rows), :]
        owner = lax.div(screen_of_level[level], per_owner)
        tiles[owner, level - starts[owner]] = jnp.where(row < rest, far_tile, near_tile)
        return carry

    half = owners // 2
    middle = starts[half]
    pairs = lax.div(middle, 2)
    lax.fori_loop(0, pairs, lambda i, c: place(2 * i + 1, place(2 * i, c)), 0)
    lax.fori_loop(2 * pairs, middle, place, 0)
    copies = [
        pltpu.make_async_copy(tiles.at[at, pl.ds(0, slots)], out.at[at], sems.at[0, n])
        for n, at in enumerate((pl.ds(0, half), pl.ds(half, half)))
    ]
    copies[0].start()
    pairs = lax.div(levels - middle, 2)
    lax.fori_loop(0, pairs, lambda i, c: place(middle + 2 * i + 1, place(middle + 2 * i, c)), 0)
    lax.fori_loop(middle + 2 * pairs, levels, place, 0)
    copies[1].start()
    most = starts[1]
    for g in range(1, owners):
        most = jnp.maximum(most, starts[g + 1] - starts[g])

    @pl.when(most > slots)
    def _():
        copy = pltpu.make_async_copy(tiles.at[:, pl.ds(slots, extra.shape[1])], extra, sems.at[1, 0])
        copy.start()
        copy.wait()

    for copy in copies:
        copy.wait()


def place_rows(here, sent, shift_rows, starts, screen_of_level, got, over, owners, rows, slots, most):
    devices = got.shape[0]
    levels = shift_rows.shape[0]
    return pl.pallas_call(
        place_rows_kernel,
        in_specs=[SCALARS] * 5 + [ANYWHERE] * 2,
        out_specs=[ANYWHERE] * 2,
        out_shape=[f32((owners, slots, rows, LANES)), f32((owners, most - slots, rows, LANES))],
        scratch_shapes=[
            pltpu.VMEM((devices * (got.shape[1] + over.shape[1]) + 2 * rows, LANES), jnp.float32),
            pltpu.VMEM((owners, most, rows, LANES), jnp.float32),
            pltpu.SMEM((devices,), jnp.int32),
            pltpu.SemaphoreType.DMA((2, devices)),
        ],
        compiler_params=params(63),
        name="place_rows",
    )(here, sent, shift_rows, starts, screen_of_level, got, over)


def sum_screens_kernel(here, starts, shift_cols, screen_of_level, got, extra, out):
    owners, slots = got.shape[:2]
    screens, rows = out.shape[:2]
    me = here[1]
    first = starts[me]
    lane = lax.broadcasted_iota(jnp.int32, (rows, LANES), 1)
    out[...] = jnp.zeros(out.shape, jnp.float32)

    def add(source, index, at):
        level = first + index
        shift = shift_cols[level]
        block, rest = shift // LANES, lax.rem(shift, LANES)
        screen = screen_of_level[level] - me * screens
        for t in range(owners):
            near = source[lax.rem(t - block + owners, owners), at]
            far = source[lax.rem(t - block - 1 + owners, owners), at]
            both = pltpu.roll(jnp.where(lane < LANES - rest, near, far), rest, 1)
            out[screen, :, t * LANES : (t + 1) * LANES] += both

    count = starts[me + 1] - first

    def body(index, carry):
        add(got, index, index)
        return carry

    def more(index, carry):
        add(extra, index, index - slots)
        return carry

    lax.fori_loop(0, jnp.minimum(count, slots), body, 0)
    lax.fori_loop(slots, jnp.maximum(count, slots), more, 0)


def sum_screens(here, starts, shift_cols, screen_of_level, got, extra, screens):
    owners, _, rows = got.shape[:3]
    return pl.pallas_call(
        sum_screens_kernel,
        in_specs=[SCALARS] * 4 + [WHOLE] * 2,
        out_specs=WHOLE,
        out_shape=f32((screens, rows, owners * LANES)),
        compiler_params=params(63),
        name="sum_screens",
    )(here, starts, shift_cols, screen_of_level, got, extra)


def swap(block, axis):
    return lax.all_to_all(block, axis, split_axis=0, concat_axis=0, tiled=True)


ROWS_AT_ONCE = 272
ROWS_MORE = 96
LEVELS_AT_ONCE = 13


def swap_more(over, first, need):
    part = ROWS_MORE
    rounds = jnp.maximum(need - first + part - 1, 0) // part

    def body(carry):
        done, over = carry
        piece = lax.dynamic_slice_in_dim(over, done * part, part, 1)
        return done + 1, lax.dynamic_update_slice_in_dim(over, swap(piece, "gx"), done * part, 1)

    return lax.while_loop(lambda carry: carry[0] < rounds, body, (jnp.int32(0), over))[1]


def swap_extra(extra, needed):
    body = lambda carry: (carry[0] - 1, swap(carry[1], "gy"))
    return lax.while_loop(lambda carry: carry[0] > 0, body, (needed.astype(jnp.int32), extra))[1]


def local(state, eddy, shift_rows, shift_cols, screen_of_level):
    levels, rows = state.shape[1:3]
    devices, owners = lax.axis_size("gx"), lax.axis_size("gy")
    per_owner = NS // owners
    most = 4 * per_owner
    here = jnp.stack([lax.axis_index("gx"), lax.axis_index("gy")]).astype(jnp.int32)

    block, rest = shift_rows // rows, shift_rows % rows
    place = jnp.arange(devices, dtype=jnp.int32)[:, None]
    rows_sent = jnp.sum(
        jnp.where(place == block[None], rows - rest[None], 0)
        + jnp.where(place == (block[None] + 1) % devices, rest[None], 0),
        axis=1,
    )
    bounds = per_owner * jnp.arange(owners + 1, dtype=jnp.int32)[:, None]
    starts = jnp.sum((screen_of_level[None] < bounds).astype(jnp.int32), axis=1)
    most_rows = jnp.max(rows_sent)
    most_levels = jnp.max(starts[1:] - starts[:-1])

    q, *edges = q_edges(state)
    q_halos = exchange(edges)

    beyond = -(-(levels * rows - ROWS_AT_ONCE) // ROWS_MORE) * ROWS_MORE
    out, over = send_rows(ROWS_AT_ONCE, beyond, devices, here, shift_rows, q, state, eddy, q_halos)
    got = swap(out, "gx")
    halos = exchange(state_edges(state, out))
    over = swap_more(over, ROWS_AT_ONCE, most_rows)
    out, extra = place_rows(
        here, rows_sent, shift_rows, starts, screen_of_level, got, over, owners, rows, LEVELS_AT_ONCE, most
    )
    out, extra, *halos = lax.optimization_barrier((out, extra, *halos))
    got = swap(out, "gy")
    advanced = advance(state, eddy, halos, q_halos, out)
    extra = swap_extra(extra, most_levels > LEVELS_AT_ONCE)
    screens = sum_screens(here, starts, shift_cols, screen_of_level, got, extra, per_owner)
    return advanced, screens


def solution(mesh):
    placed = (P(None, None, "gx", "gy"), P(None, "gx", "gy"), P(), P(), P())
    return jax.shard_map(
        local,
        mesh=mesh,
        in_specs=placed,
        out_specs=(P(None, None, "gx", "gy"), P("gy", "gx", None)),
        check_vma=False,
    )
```

```python
import functools

import jax
import jax.numpy as jnp
import ml_dtypes
import numpy as np
from jax import lax
from jax.experimental import pallas as pl
from jax.experimental.pallas import tpu as pltpu
from jax.sharding import PartitionSpec as P

NS = 32

time_step = 0.1
buoyancy_gain = 0.3
heat_weight = -0.79
moist_weight = 0.56

LANES = 128
GROUP = 32
WHOLE = pl.BlockSpec(memory_space=pltpu.VMEM)
SCALARS = pl.BlockSpec(memory_space=pltpu.SMEM)
ANYWHERE = pl.BlockSpec(memory_space=pl.ANY)


def params(mebibytes):
    return pltpu.CompilerParams(vmem_limit_bytes=mebibytes * 1024 * 1024)


def f32(shape):
    return jax.ShapeDtypeStruct(shape, jnp.float32)


def pack_edges(value, count, rows, outs):
    top, bottom, low, high = outs
    lane = lax.broadcasted_iota(jnp.int32, (rows, LANES), 1)
    low_acc = jnp.zeros((rows, LANES), jnp.float32)
    high_acc = low_acc
    for level in range(count):
        tile = value(level)
        top[3 * level : 3 * level + 3] = tile[0:3]
        bottom[3 * level : 3 * level + 3] = tile[rows - 3 : rows]
        turned = pltpu.roll(tile, 3 * level, 1)
        place = lane - 3 * level
        low_acc = jnp.where((place >= 0) & (place < 3), turned, low_acc)
        high_acc = jnp.where(((place >= -3) & (place < 0)) | (place >= 125), turned, high_acc)
    low[0] = low_acc
    high[0] = high_acc


def q_edges_kernel(heat, moist, q, *outs):
    rows = q.shape[1]

    def value(level):
        tile = heat_weight * heat[0, level] + moist_weight * moist[0, level]
        q[level] = tile
        return tile

    pack_edges(value, q.shape[0], rows, outs)


def state_edges_kernel(after, state, top, bottom, low, high):
    levels, rows = state.shape[1:3]
    for group in range(levels // GROUP):
        first = group * GROUP
        strip = pl.ds(3 * first, 3 * GROUP)
        one = pl.ds(group, 1)
        outs = (top.at[strip], bottom.at[strip], low.at[one], high.at[one])
        pack_edges(lambda level: state[0, first + level], GROUP, rows, outs)


def edge_outputs(fields, levels, rows):
    groups = levels // GROUP
    shapes = [f32((fields * levels * 3, LANES))] * 2 + [f32((fields * groups, rows, LANES))] * 2
    return shapes, groups


def q_edges(state):
    levels, rows = state.shape[1:3]
    shapes, groups = edge_outputs(1, levels, rows)
    member = lambda n: pl.BlockSpec((1, GROUP, rows, LANES), lambda i: (n, i, 0, 0))
    return pl.pallas_call(
        q_edges_kernel,
        grid=(groups,),
        in_specs=[member(3), member(4)],
        out_specs=[pl.BlockSpec((GROUP, rows, LANES), lambda i: (i, 0, 0))]
        + [pl.BlockSpec((3 * GROUP, LANES), lambda i: (i, 0))] * 2
        + [pl.BlockSpec((1, rows, LANES), lambda i: (i, 0, 0))] * 2,
        out_shape=[f32((levels, rows, LANES))] + shapes,
        compiler_params=params(63),
        name="q_edges",
    )(state, state)


def state_edges(state, after):
    levels, rows = state.shape[1:3]
    fields = 4
    shapes, groups = edge_outputs(fields, levels, rows)
    return pl.pallas_call(
        state_edges_kernel,
        grid=(fields,),
        in_specs=[ANYWHERE, pl.BlockSpec((1, levels, rows, LANES), lambda m: (m, 0, 0, 0))],
        out_specs=[pl.BlockSpec((3 * levels, LANES), lambda m: (m, 0))] * 2
        + [pl.BlockSpec((groups, rows, LANES), lambda m: (m, 0, 0))] * 2,
        out_shape=shapes,
        compiler_params=params(63),
        cost_estimate=pl.CostEstimate(flops=0, bytes_accessed=60_000_000, transcendentals=0),
        name="state_edges",
    )(after, state)


def ring(axis, step):
    count = lax.axis_size(axis)
    return [(i, (i + step) % count) for i in range(count)]


def exchange(edges):
    top, bottom, low, high = edges
    left = lax.ppermute(high, "gy", ring("gy", 1))
    right = lax.ppermute(low, "gy", ring("gy", -1))
    above = lax.ppermute(bottom, "gx", ring("gx", 1))
    below = lax.ppermute(top, "gx", ring("gx", -1))
    return above, below, left, right


def factors(wind, eddy):
    scale = time_step / 60.0
    winds = [wind(n) * scale for n in range(3)]
    sizes = [jnp.abs(w) for w in winds]
    mix = time_step * eddy
    keep = 1.0 - 6.0 * mix - 20.0 * (sizes[0] + sizes[1] + sizes[2])
    return winds, sizes, mix, keep


def along(near, wind, size):
    m3, m2, m1, p1, p2, p3 = near
    first = p1 + m1
    central = (p3 - m3) - 9.0 * (p2 - m2) + 45.0 * (p1 - m1)
    spread = (p3 + m3) - 6.0 * (p2 + m2) + 15.0 * first
    return first, size * spread - wind * central


SIDES = (-3, -2, -1, 1, 2, 3)
ROWS = 8


def fill_pad(tile, row_at, above, below, pad):
    rows = tile.shape[0]
    pad[8 : 8 + rows] = tile
    pad[5:8] = above[pl.ds(row_at, 3), :]
    pad[8 + rows : 11 + rows] = below[pl.ds(row_at, 3), :]


def step_rows(field, level, levels, at, group, back, left, right, pad, coefficients):
    winds, sizes, mix, keep = coefficients
    tile = field(level)
    east = [pad[8 + at + n : 8 + at + n + ROWS] for n in SIDES]
    lane = lax.broadcasted_iota(jnp.int32, (ROWS, LANES), 1)
    low, high = left[group, at : at + ROWS], right[group, at : at + ROWS]
    edge = jnp.where(lane < 64, pltpu.roll(high, back, 1), pltpu.roll(low, back, 1))
    north = [pltpu.roll(jnp.where(lane >= LANES - n, edge, tile), n, 1) for n in (3, 2, 1)]
    north += [pltpu.roll(jnp.where(lane < n, edge, tile), LANES - n, 1) for n in (1, 2, 3)]
    upward = [field(jnp.clip(level + n, 0, levels - 1)) for n in SIDES]
    total, result = 0.0, tile * keep
    for near, wind, size in zip((east, north, upward), winds, sizes):
        first, moved = along(near, wind, size)
        total = total + first
        result = result + moved
    return result + mix * total


def lane_place(level):
    return level // GROUP, lax.rem(LANES - 3 * lax.rem(level, GROUP), LANES)


def lane_weights():
    inside = np.zeros((LANES, 3, LANES), np.float32)
    beyond = np.zeros((LANES, 3, LANES), np.float32)
    for j in range(LANES):
        for n, terms in ((1, (1, 45, 15)), (2, (0, -9, -6)), (3, (0, 1, 1))):
            for sign in (1, -1):
                source = j + sign * n
                where = inside if 0 <= source < LANES else beyond
                for which in range(3):
                    factor = terms[which] * (sign if which == 1 else 1)
                    where[source % LANES, which, j] += factor
    inside, beyond = inside.reshape(LANES, -1), beyond.reshape(LANES, -1)
    return np.concatenate([inside, inside, beyond, beyond]).astype(ml_dtypes.bfloat16)


def halves(tile):
    high = tile.astype(jnp.bfloat16)
    return high, (tile - high.astype(jnp.float32)).astype(jnp.bfloat16)


PAIR = 4
CHUNK = 8


def advance_kernel(chunk, *refs):
    state, eddy, above, below, left, right, *others, weights, after, out, pad, even, odd = refs[:-4]
    moist = refs[-4:]
    fields, levels, rows = state.shape[:3]
    groups = levels // GROUP
    base = pl.program_id(0) * chunk
    lane = lax.broadcasted_iota(jnp.int32, (rows, LANES), 1)

    def multiply(start, product):
        parts = []
        for one in range(PAIR):
            level = jnp.minimum(start + one, levels - 1)
            group, back = lane_place(level)
            for member in range(fields):
                last = member == fields - 1
                at = group if last else member * groups + group
                high = pltpu.roll((moist[3] if last else right)[at], back, 1)
                low = pltpu.roll((moist[2] if last else left)[at], back, 1)
                edge = jnp.where(lane < 3, high, jnp.where(lane >= LANES - 3, low, 0.0))
                parts.append(jnp.concatenate(halves(state[member, level]) + halves(edge), axis=1))
        product[...] = jnp.dot(
            jnp.concatenate(parts, axis=0), weights[...], preferred_element_type=jnp.float32
        )

    def finish(step, product):
        for one in range(PAIR):
            index = step * PAIR + one
            level = base + index
            for member in range(fields):
                last = member == fields - 1
                fill_pad(
                    state[member, level],
                    3 * level if last else 3 * (member * levels + level),
                    moist[0] if last else above,
                    moist[1] if last else below,
                    pad.at[one, member],
                )
            for at in range(0, rows, ROWS):
                here = slice(at, at + ROWS)
                winds, sizes, mix, keep = factors(lambda n: state[n, level, here], eddy[level, here])
                for member in range(fields):
                    tile = state[member, level, here]
                    east = [pad[one, member, 8 + at + n : 8 + at + n + ROWS] for n in SIDES]
                    upward = [state[member, jnp.clip(level + n, 0, levels - 1), here] for n in SIDES]
                    spot = (one * fields + member) * rows + at
                    spot = slice(spot, spot + ROWS)
                    total = product[spot, 0:LANES]
                    result = tile * keep + (
                        sizes[1] * product[spot, 2 * LANES : 3 * LANES]
                        - winds[1] * product[spot, LANES : 2 * LANES]
                    )
                    for near, axis in ((east, 0), (upward, 2)):
                        first, moved = along(near, winds[axis], sizes[axis])
                        total = total + first
                        result = result + moved
                    result = result + mix * total
                    if member == 2:
                        result = result + (time_step * buoyancy_gain) * state[3, level, here]
                    out[member, index, here] = result

    @pl.when(pl.program_id(0) == 0)
    def _():
        for mine, heat, both in zip(moist, (above, below, left, right), others):
            length = mine.shape[0]
            fourth = heat[pl.ds(3 * length, length)]
            mine[...] = (both[...] - heat_weight * fourth) * (1.0 / moist_weight)
        multiply(0, even)

    def body(twice, carry):
        step = 2 * twice
        multiply(base + (step + 1) * PAIR, odd)
        finish(step, even)
        multiply(base + (step + 2) * PAIR, even)
        finish(step + 1, odd)
        return carry

    lax.fori_loop(0, chunk // PAIR // 2, body, 0)


def advance(state, eddy, halos, q_halos, after):
    fields, levels, rows = state.shape[:3]
    chunk = CHUNK
    return pl.pallas_call(
        functools.partial(advance_kernel, chunk),
        grid=(levels // chunk,),
        in_specs=[WHOLE] * 11 + [ANYWHERE],
        out_specs=pl.BlockSpec((fields, chunk, rows, LANES), lambda i: (0, i, 0, 0)),
        out_shape=f32(state.shape),
        scratch_shapes=[
            pltpu.VMEM((PAIR, fields, rows + 16, LANES), jnp.float32),
            pltpu.VMEM((PAIR * fields * rows, 3 * LANES), jnp.float32),
            pltpu.VMEM((PAIR * fields * rows, 3 * LANES), jnp.float32),
        ]
        + [pltpu.VMEM(h.shape, jnp.float32) for h in q_halos],
        compiler_params=params(63),
        cost_estimate=pl.CostEstimate(
            flops=0, bytes_accessed=200_000_000, transcendentals=0
        ),
        name="advance",
    )(state, eddy, *halos, *q_halos, jnp.asarray(lane_weights()), after)


def row_places(shift_rows, filled, level, rows, devices):
    shift = shift_rows[level]
    block, rest = lax.div(shift, rows), lax.rem(shift, rows)
    after = lax.select(block == devices - 1, 0, block + 1)
    near = filled[block]
    filled[block] = near + rows - rest
    far = filled[after]
    filled[after] = far + rest
    return block, after, rest, near, far


UNROLL = 4


def send_rows_kernel(chunk, here, shift_rows, q, wind, eddy, *refs):
    above, below, left, right, out, over, packed, pad, double, filled, sems = refs
    levels, rows = q.shape[:2]
    devices, capacity = out.shape[:2]
    stride = capacity + over.shape[1] + rows
    base = pl.program_id(0) * chunk

    @pl.when(pl.program_id(0) == 0)
    def _():
        for d in range(devices):
            filled[d] = 0

    def one(index, slot):
        level = base + index
        group, back = lane_place(level)
        ready = double.at[slot]
        fill_pad(q[level], 3 * level, above, below, pad.at[slot])
        for at in range(0, rows, ROWS):
            strip = slice(at, at + ROWS)
            coefficients = factors(lambda n: wind[n, index, strip], eddy[index, strip])
            ready[strip] = step_rows(
                lambda k: q[k, strip], level, levels, at, group, back, left, right, pad.at[slot], coefficients
            )

    def body(step, carry):
        for slot in range(UNROLL):
            one(step * UNROLL + slot, slot)
        for slot in range(UNROLL):
            ready = double.at[slot]
            level = base + step * UNROLL + slot
            block, after, rest, near, far = row_places(shift_rows, filled, level, rows, devices)
            packed[pl.ds(block * stride + near, rows), :] = ready[0:rows]
            packed[pl.ds(after * stride + far, rows), :] = ready[pl.ds(rows - rest, rows), :]
        return carry

    lax.fori_loop(0, chunk // UNROLL, body, 0)

    @pl.when(pl.program_id(0) == pl.num_programs(0) - 1)
    def _():
        copies = [
            pltpu.make_async_copy(
                packed.at[pl.ds(d * stride, capacity)], out.at[lax.rem(here[0] + d, devices)], sems.at[0, d]
            )
            for d in range(devices)
        ]
        for copy in copies:
            copy.start()
        for copy in copies:
            copy.wait()
        for d in range(devices):

            @pl.when(filled[d] > capacity)
            def _():
                copy = pltpu.make_async_copy(
                    packed.at[pl.ds(d * stride + capacity, over.shape[1])],
                    over.at[lax.rem(here[0] + d, devices)],
                    sems.at[1, d],
                )
                copy.start()
                copy.wait()


def send_rows(capacity, beyond, devices, here, shift_rows, q, state, eddy, halos):
    levels, rows = q.shape[:2]
    chunk = 16
    return pl.pallas_call(
        functools.partial(send_rows_kernel, chunk),
        grid=(levels // chunk,),
        in_specs=[
            SCALARS,
            SCALARS,
            WHOLE,
            pl.BlockSpec((3, chunk, rows, LANES), lambda i: (0, i, 0, 0)),
            pl.BlockSpec((chunk, rows, LANES), lambda i: (i, 0, 0)),
        ]
        + [WHOLE] * 4,
        out_specs=[ANYWHERE] * 2,
        out_shape=[
            f32((devices, capacity, LANES)),
            f32((devices, beyond, LANES)),
        ],
        scratch_shapes=[
            pltpu.VMEM((devices * (capacity + beyond + rows), LANES), jnp.float32),
            pltpu.VMEM((UNROLL, rows + 16, LANES), jnp.float32),
            pltpu.VMEM((UNROLL, 2 * rows, LANES), jnp.float32),
            pltpu.SMEM((devices,), jnp.int32),
            pltpu.SemaphoreType.DMA((2, devices)),
        ],
        compiler_params=params(63),
        name="send_rows",
    )(here, shift_rows, q, state, eddy, *halos)


def place_rows_kernel(here, sent, shift_rows, starts, screen_of_level, got, over, out, extra, held, tiles, filled, sems):
    devices, capacity = got.shape[:2]
    owners, slots, rows = out.shape[:3]
    levels = shift_rows.shape[0]
    stride = capacity + over.shape[1]
    per_owner = NS // owners
    me = here[0]
    copies = [
        pltpu.make_async_copy(got.at[d], held.at[pl.ds(rows + d * stride, capacity)], sems.at[0, d])
        for d in range(devices)
    ]
    for copy in copies:
        copy.start()
    for d in range(devices):
        filled[d] = 0
    for copy in copies:
        copy.wait()
    for d in range(devices):

        @pl.when(sent[lax.rem(me - d + devices, devices)] > capacity)
        def _():
            copy = pltpu.make_async_copy(
                over.at[d], held.at[pl.ds(rows + d * stride + capacity, over.shape[1])], sems.at[1, d]
            )
            copy.start()
            copy.wait()

    row = lax.broadcasted_iota(jnp.int32, (rows, LANES), 0)

    def place(level, carry):
        block, after, rest, near, far = row_places(shift_rows, filled, level, rows, devices)
        near_from = lax.select(me >= block, me - block, me - block + devices)
        far_from = lax.select(me >= after, me - after, me - after + devices)
        near_tile = held[pl.ds(rows + near_from * stride + near - rest, rows), :]
        far_tile = held[pl.ds(rows + far_from * stride + far, rows), :]
        owner = lax.div(screen_of_level[level], per_owner)
        tiles[owner, level - starts[owner]] = jnp.where(row < rest, far_tile, near_tile)
        return carry

    half = owners // 2
    middle = starts[half]
    pairs = lax.div(middle, 2)
    lax.fori_loop(0, pairs, lambda i, c: place(2 * i + 1, place(2 * i, c)), 0)
    lax.fori_loop(2 * pairs, middle, place, 0)
    copies = [
        pltpu.make_async_copy(tiles.at[at, pl.ds(0, slots)], out.at[at], sems.at[0, n])
        for n, at in enumerate((pl.ds(0, half), pl.ds(half, half)))
    ]
    copies[0].start()
    pairs = lax.div(levels - middle, 2)
    lax.fori_loop(0, pairs, lambda i, c: place(middle + 2 * i + 1, place(middle + 2 * i, c)), 0)
    lax.fori_loop(middle + 2 * pairs, levels, place, 0)
    copies[1].start()
    most = starts[1]
    for g in range(1, owners):
        most = jnp.maximum(most, starts[g + 1] - starts[g])

    @pl.when(most > slots)
    def _():
        copy = pltpu.make_async_copy(tiles.at[:, pl.ds(slots, extra.shape[1])], extra, sems.at[1, 0])
        copy.start()
        copy.wait()

    for copy in copies:
        copy.wait()


def place_rows(here, sent, shift_rows, starts, screen_of_level, got, over, owners, rows, slots, most):
    devices = got.shape[0]
    levels = shift_rows.shape[0]
    return pl.pallas_call(
        place_rows_kernel,
        in_specs=[SCALARS] * 5 + [ANYWHERE] * 2,
        out_specs=[ANYWHERE] * 2,
        out_shape=[f32((owners, slots, rows, LANES)), f32((owners, most - slots, rows, LANES))],
        scratch_shapes=[
            pltpu.VMEM((devices * (got.shape[1] + over.shape[1]) + 2 * rows, LANES), jnp.float32),
            pltpu.VMEM((owners, most, rows, LANES), jnp.float32),
            pltpu.SMEM((devices,), jnp.int32),
            pltpu.SemaphoreType.DMA((2, devices)),
        ],
        compiler_params=params(63),
        name="place_rows",
    )(here, sent, shift_rows, starts, screen_of_level, got, over)


def sum_screens_kernel(here, starts, shift_cols, screen_of_level, got, extra, out):
    owners, slots = got.shape[:2]
    screens, rows = out.shape[:2]
    me = here[1]
    first = starts[me]
    lane = lax.broadcasted_iota(jnp.int32, (rows, LANES), 1)
    out[...] = jnp.zeros(out.shape, jnp.float32)

    def add(source, index, at):
        level = first + index
        shift = shift_cols[level]
        block, rest = shift // LANES, lax.rem(shift, LANES)
        screen = screen_of_level[level] - me * screens
        for t in range(owners):
            near = source[lax.rem(t - block + owners, owners), at]
            far = source[lax.rem(t - block - 1 + owners, owners), at]
            both = pltpu.roll(jnp.where(lane < LANES - rest, near, far), rest, 1)
            out[screen, :, t * LANES : (t + 1) * LANES] += both

    count = starts[me + 1] - first

    def body(index, carry):
        add(got, index, index)
        return carry

    def more(index, carry):
        add(extra, index, index - slots)
        return carry

    lax.fori_loop(0, jnp.minimum(count, slots), body, 0)
    lax.fori_loop(slots, jnp.maximum(count, slots), more, 0)


def sum_screens(here, starts, shift_cols, screen_of_level, got, extra, screens):
    owners, _, rows = got.shape[:3]
    return pl.pallas_call(
        sum_screens_kernel,
        in_specs=[SCALARS] * 4 + [WHOLE] * 2,
        out_specs=WHOLE,
        out_shape=f32((screens, rows, owners * LANES)),
        compiler_params=params(63),
        name="sum_screens",
    )(here, starts, shift_cols, screen_of_level, got, extra)


def swap(block, axis):
    return lax.all_to_all(block, axis, split_axis=0, concat_axis=0, tiled=True)


ROWS_AT_ONCE = 264
ROWS_MORE = 48
LEVELS_AT_ONCE = 13


def swap_more(over, first, need):
    part = ROWS_MORE
    rounds = jnp.maximum(need - first + part - 1, 0) // part

    def body(carry):
        done, over = carry
        piece = lax.dynamic_slice_in_dim(over, done * part, part, 1)
        return done + 1, lax.dynamic_update_slice_in_dim(over, swap(piece, "gx"), done * part, 1)

    return lax.while_loop(lambda carry: carry[0] < rounds, body, (jnp.int32(0), over))[1]


def swap_extra(extra, needed):
    body = lambda carry: (carry[0] - 1, swap(carry[1], "gy"))
    return lax.while_loop(lambda carry: carry[0] > 0, body, (needed.astype(jnp.int32), extra))[1]


def local(state, eddy, shift_rows, shift_cols, screen_of_level):
    levels, rows = state.shape[1:3]
    devices, owners = lax.axis_size("gx"), lax.axis_size("gy")
    per_owner = NS // owners
    most = 4 * per_owner
    here = jnp.stack([lax.axis_index("gx"), lax.axis_index("gy")]).astype(jnp.int32)

    block, rest = shift_rows // rows, shift_rows % rows
    place = jnp.arange(devices, dtype=jnp.int32)[:, None]
    rows_sent = jnp.sum(
        jnp.where(place == block[None], rows - rest[None], 0)
        + jnp.where(place == (block[None] + 1) % devices, rest[None], 0),
        axis=1,
    )
    bounds = per_owner * jnp.arange(owners + 1, dtype=jnp.int32)[:, None]
    starts = jnp.sum((screen_of_level[None] < bounds).astype(jnp.int32), axis=1)
    most_rows = jnp.max(rows_sent)
    most_levels = jnp.max(starts[1:] - starts[:-1])

    q, *edges = q_edges(state)
    q_halos = exchange(edges)

    beyond = -(-(levels * rows - ROWS_AT_ONCE) // ROWS_MORE) * ROWS_MORE
    out, over = send_rows(ROWS_AT_ONCE, beyond, devices, here, shift_rows, q, state, eddy, q_halos)
    got = swap(out, "gx")
    halos = exchange(state_edges(state, out))
    over = swap_more(over, ROWS_AT_ONCE, most_rows)
    out, extra = place_rows(
        here, rows_sent, shift_rows, starts, screen_of_level, got, over, owners, rows, LEVELS_AT_ONCE, most
    )
    out, extra, *halos = lax.optimization_barrier((out, extra, *halos))
    got = swap(out, "gy")
    advanced = advance(state, eddy, halos, q_halos, out)
    extra = swap_extra(extra, most_levels > LEVELS_AT_ONCE)
    screens = sum_screens(here, starts, shift_cols, screen_of_level, got, extra, per_owner)
    return advanced, screens


def solution(mesh):
    placed = (P(None, None, "gx", "gy"), P(None, "gx", "gy"), P(), P(), P())
    return jax.shard_map(
        local,
        mesh=mesh,
        in_specs=placed,
        out_specs=(P(None, None, "gx", "gy"), P("gy", "gx", None)),
        check_vma=False,
    )
```

```python
import functools

import jax
import jax.numpy as jnp
import ml_dtypes
import numpy as np
from jax import lax
from jax.experimental import pallas as pl
from jax.experimental.pallas import tpu as pltpu
from jax.sharding import PartitionSpec as P

NS = 32

time_step = 0.1
buoyancy_gain = 0.3
heat_weight = -0.79
moist_weight = 0.56

LANES = 128
GROUP = 32
WHOLE = pl.BlockSpec(memory_space=pltpu.VMEM)
SCALARS = pl.BlockSpec(memory_space=pltpu.SMEM)
ANYWHERE = pl.BlockSpec(memory_space=pl.ANY)


def params(mebibytes):
    return pltpu.CompilerParams(vmem_limit_bytes=mebibytes * 1024 * 1024)


def f32(shape):
    return jax.ShapeDtypeStruct(shape, jnp.float32)


def pack_edges(value, count, rows, outs):
    top, bottom, low, high = outs
    lane = lax.broadcasted_iota(jnp.int32, (rows, LANES), 1)
    low_acc = jnp.zeros((rows, LANES), jnp.float32)
    high_acc = low_acc
    for level in range(count):
        tile = value(level)
        top[3 * level : 3 * level + 3] = tile[0:3]
        bottom[3 * level : 3 * level + 3] = tile[rows - 3 : rows]
        turned = pltpu.roll(tile, 3 * level, 1)
        place = lane - 3 * level
        low_acc = jnp.where((place >= 0) & (place < 3), turned, low_acc)
        high_acc = jnp.where(((place >= -3) & (place < 0)) | (place >= 125), turned, high_acc)
    low[0] = low_acc
    high[0] = high_acc


def q_edges_kernel(heat, moist, q, *outs):
    rows = q.shape[1]

    def value(level):
        tile = heat_weight * heat[0, level] + moist_weight * moist[0, level]
        q[level] = tile
        return tile

    pack_edges(value, q.shape[0], rows, outs)


def state_edges_kernel(after, state, top, bottom, low, high):
    levels, rows = state.shape[1:3]
    for group in range(levels // GROUP):
        first = group * GROUP
        strip = pl.ds(3 * first, 3 * GROUP)
        one = pl.ds(group, 1)
        outs = (top.at[strip], bottom.at[strip], low.at[one], high.at[one])
        pack_edges(lambda level: state[0, first + level], GROUP, rows, outs)


def edge_outputs(fields, levels, rows):
    groups = levels // GROUP
    shapes = [f32((fields * levels * 3, LANES))] * 2 + [f32((fields * groups, rows, LANES))] * 2
    return shapes, groups


def q_edges(state):
    levels, rows = state.shape[1:3]
    shapes, groups = edge_outputs(1, levels, rows)
    member = lambda n: pl.BlockSpec((1, GROUP, rows, LANES), lambda i: (n, i, 0, 0))
    return pl.pallas_call(
        q_edges_kernel,
        grid=(groups,),
        in_specs=[member(3), member(4)],
        out_specs=[pl.BlockSpec((GROUP, rows, LANES), lambda i: (i, 0, 0))]
        + [pl.BlockSpec((3 * GROUP, LANES), lambda i: (i, 0))] * 2
        + [pl.BlockSpec((1, rows, LANES), lambda i: (i, 0, 0))] * 2,
        out_shape=[f32((levels, rows, LANES))] + shapes,
        compiler_params=params(63),
        name="q_edges",
    )(state, state)


def state_edges(state, after):
    levels, rows = state.shape[1:3]
    fields = 4
    shapes, groups = edge_outputs(fields, levels, rows)
    return pl.pallas_call(
        state_edges_kernel,
        grid=(fields,),
        in_specs=[ANYWHERE, pl.BlockSpec((1, levels, rows, LANES), lambda m: (m, 0, 0, 0))],
        out_specs=[pl.BlockSpec((3 * levels, LANES), lambda m: (m, 0))] * 2
        + [pl.BlockSpec((groups, rows, LANES), lambda m: (m, 0, 0))] * 2,
        out_shape=shapes,
        compiler_params=params(63),
        cost_estimate=pl.CostEstimate(flops=0, bytes_accessed=60_000_000, transcendentals=0),
        name="state_edges",
    )(after, state)


def ring(axis, step):
    count = lax.axis_size(axis)
    return [(i, (i + step) % count) for i in range(count)]


def exchange(edges):
    top, bottom, low, high = edges
    left = lax.ppermute(high, "gy", ring("gy", 1))
    right = lax.ppermute(low, "gy", ring("gy", -1))
    above = lax.ppermute(bottom, "gx", ring("gx", 1))
    below = lax.ppermute(top, "gx", ring("gx", -1))
    return above, below, left, right


def factors(wind, eddy):
    scale = time_step / 60.0
    winds = [wind(n) * scale for n in range(3)]
    sizes = [jnp.abs(w) for w in winds]
    mix = time_step * eddy
    keep = 1.0 - 6.0 * mix - 20.0 * (sizes[0] + sizes[1] + sizes[2])
    return winds, sizes, mix, keep


def along(near, wind, size):
    m3, m2, m1, p1, p2, p3 = near
    first = p1 + m1
    central = (p3 - m3) - 9.0 * (p2 - m2) + 45.0 * (p1 - m1)
    spread = (p3 + m3) - 6.0 * (p2 + m2) + 15.0 * first
    return first, size * spread - wind * central


SIDES = (-3, -2, -1, 1, 2, 3)
ROWS = 8


def fill_pad(tile, row_at, above, below, pad):
    rows = tile.shape[0]
    pad[8 : 8 + rows] = tile
    pad[5:8] = above[pl.ds(row_at, 3), :]
    pad[8 + rows : 11 + rows] = below[pl.ds(row_at, 3), :]


def step_rows(field, level, levels, at, group, back, left, right, pad, coefficients):
    winds, sizes, mix, keep = coefficients
    tile = field(level)
    east = [pad[8 + at + n : 8 + at + n + ROWS] for n in SIDES]
    lane = lax.broadcasted_iota(jnp.int32, (ROWS, LANES), 1)
    low, high = left[group, at : at + ROWS], right[group, at : at + ROWS]
    edge = jnp.where(lane < 64, pltpu.roll(high, back, 1), pltpu.roll(low, back, 1))
    north = [pltpu.roll(jnp.where(lane >= LANES - n, edge, tile), n, 1) for n in (3, 2, 1)]
    north += [pltpu.roll(jnp.where(lane < n, edge, tile), LANES - n, 1) for n in (1, 2, 3)]
    upward = [field(jnp.clip(level + n, 0, levels - 1)) for n in SIDES]
    total, result = 0.0, tile * keep
    for near, wind, size in zip((east, north, upward), winds, sizes):
        first, moved = along(near, wind, size)
        total = total + first
        result = result + moved
    return result + mix * total


def lane_place(level):
    return level // GROUP, lax.rem(LANES - 3 * lax.rem(level, GROUP), LANES)


def lane_weights():
    inside = np.zeros((LANES, 3, LANES), np.float32)
    beyond = np.zeros((LANES, 3, LANES), np.float32)
    for j in range(LANES):
        for n, terms in ((1, (1, 45, 15)), (2, (0, -9, -6)), (3, (0, 1, 1))):
            for sign in (1, -1):
                source = j + sign * n
                where = inside if 0 <= source < LANES else beyond
                for which in range(3):
                    factor = terms[which] * (sign if which == 1 else 1)
                    where[source % LANES, which, j] += factor
    inside, beyond = inside.reshape(LANES, -1), beyond.reshape(LANES, -1)
    return np.concatenate([inside, inside, beyond, beyond]).astype(ml_dtypes.bfloat16)


def halves(tile):
    high = tile.astype(jnp.bfloat16)
    return high, (tile - high.astype(jnp.float32)).astype(jnp.bfloat16)


PAIR = 4
CHUNK = 8


def advance_kernel(chunk, *refs):
    state, eddy, above, below, left, right, *others, weights, after, out, pad, even, odd = refs[:-4]
    moist = refs[-4:]
    fields, levels, rows = state.shape[:3]
    groups = levels // GROUP
    base = pl.program_id(0) * chunk
    lane = lax.broadcasted_iota(jnp.int32, (rows, LANES), 1)

    def multiply(start, product):
        parts = []
        for one in range(PAIR):
            level = jnp.minimum(start + one, levels - 1)
            group, back = lane_place(level)
            for member in range(fields):
                last = member == fields - 1
                at = group if last else member * groups + group
                high = pltpu.roll((moist[3] if last else right)[at], back, 1)
                low = pltpu.roll((moist[2] if last else left)[at], back, 1)
                edge = jnp.where(lane < 3, high, jnp.where(lane >= LANES - 3, low, 0.0))
                parts.append(jnp.concatenate(halves(state[member, level]) + halves(edge), axis=1))
        product[...] = jnp.dot(
            jnp.concatenate(parts, axis=0), weights[...], preferred_element_type=jnp.float32
        )

    def finish(step, product):
        for one in range(PAIR):
            index = step * PAIR + one
            level = base + index
            for member in range(fields):
                last = member == fields - 1
                fill_pad(
                    state[member, level],
                    3 * level if last else 3 * (member * levels + level),
                    moist[0] if last else above,
                    moist[1] if last else below,
                    pad.at[one, member],
                )
            for at in range(0, rows, ROWS):
                here = slice(at, at + ROWS)
                winds, sizes, mix, keep = factors(lambda n: state[n, level, here], eddy[level, here])
                for member in range(fields):
                    tile = state[member, level, here]
                    east = [pad[one, member, 8 + at + n : 8 + at + n + ROWS] for n in SIDES]
                    upward = [state[member, jnp.clip(level + n, 0, levels - 1), here] for n in SIDES]
                    spot = (one * fields + member) * rows + at
                    spot = slice(spot, spot + ROWS)
                    total = product[spot, 0:LANES]
                    result = tile * keep + (
                        sizes[1] * product[spot, 2 * LANES : 3 * LANES]
                        - winds[1] * product[spot, LANES : 2 * LANES]
                    )
                    for near, axis in ((east, 0), (upward, 2)):
                        first, moved = along(near, winds[axis], sizes[axis])
                        total = total + first
                        result = result + moved
                    result = result + mix * total
                    if member == 2:
                        result = result + (time_step * buoyancy_gain) * state[3, level, here]
                    out[member, index, here] = result

    @pl.when(pl.program_id(0) == 0)
    def _():
        for mine, heat, both in zip(moist, (above, below, left, right), others):
            length = mine.shape[0]
            fourth = heat[pl.ds(3 * length, length)]
            mine[...] = (both[...] - heat_weight * fourth) * (1.0 / moist_weight)
        multiply(0, even)

    def body(twice, carry):
        step = 2 * twice
        multiply(base + (step + 1) * PAIR, odd)
        finish(step, even)
        multiply(base + (step + 2) * PAIR, even)
        finish(step + 1, odd)
        return carry

    lax.fori_loop(0, chunk // PAIR // 2, body, 0)


def advance(state, eddy, halos, q_halos, after):
    fields, levels, rows = state.shape[:3]
    chunk = CHUNK
    return pl.pallas_call(
        functools.partial(advance_kernel, chunk),
        grid=(levels // chunk,),
        in_specs=[WHOLE] * 11 + [ANYWHERE],
        out_specs=pl.BlockSpec((fields, chunk, rows, LANES), lambda i: (0, i, 0, 0)),
        out_shape=f32(state.shape),
        scratch_shapes=[
            pltpu.VMEM((PAIR, fields, rows + 16, LANES), jnp.float32),
            pltpu.VMEM((PAIR * fields * rows, 3 * LANES), jnp.float32),
            pltpu.VMEM((PAIR * fields * rows, 3 * LANES), jnp.float32),
        ]
        + [pltpu.VMEM(h.shape, jnp.float32) for h in q_halos],
        compiler_params=params(63),
        cost_estimate=pl.CostEstimate(
            flops=0, bytes_accessed=200_000_000, transcendentals=0
        ),
        name="advance",
    )(state, eddy, *halos, *q_halos, jnp.asarray(lane_weights()), after)


def row_places(shift_rows, filled, level, rows, devices):
    shift = shift_rows[level]
    block, rest = lax.div(shift, rows), lax.rem(shift, rows)
    after = lax.select(block == devices - 1, 0, block + 1)
    near = filled[block]
    filled[block] = near + rows - rest
    far = filled[after]
    filled[after] = far + rest
    return block, after, rest, near, far


UNROLL = 4


def send_rows_kernel(chunk, here, shift_rows, q, wind, eddy, *refs):
    above, below, left, right, out, over, packed, pad, double, filled, sems = refs
    levels, rows = q.shape[:2]
    devices, capacity = out.shape[:2]
    stride = capacity + over.shape[1] + rows
    base = pl.program_id(0) * chunk

    @pl.when(pl.program_id(0) == 0)
    def _():
        for d in range(devices):
            filled[d] = 0

    def one(index, slot):
        level = base + index
        group, back = lane_place(level)
        ready = double.at[slot]
        fill_pad(q[level], 3 * level, above, below, pad.at[slot])
        for at in range(0, rows, ROWS):
            strip = slice(at, at + ROWS)
            coefficients = factors(lambda n: wind[n, index, strip], eddy[index, strip])
            ready[strip] = step_rows(
                lambda k: q[k, strip], level, levels, at, group, back, left, right, pad.at[slot], coefficients
            )

    def body(step, carry):
        for slot in range(UNROLL):
            one(step * UNROLL + slot, slot)
        for slot in range(UNROLL):
            ready = double.at[slot]
            level = base + step * UNROLL + slot
            block, after, rest, near, far = row_places(shift_rows, filled, level, rows, devices)
            packed[pl.ds(block * stride + near, rows), :] = ready[0:rows]
            packed[pl.ds(after * stride + far, rows), :] = ready[pl.ds(rows - rest, rows), :]
        return carry

    lax.fori_loop(0, chunk // UNROLL, body, 0)

    @pl.when(pl.program_id(0) == pl.num_programs(0) - 1)
    def _():
        copies = [
            pltpu.make_async_copy(
                packed.at[pl.ds(d * stride, capacity)], out.at[lax.rem(here[0] + d, devices)], sems.at[0, d]
            )
            for d in range(devices)
        ]
        for copy in copies:
            copy.start()
        for copy in copies:
            copy.wait()
        for d in range(devices):

            @pl.when(filled[d] > capacity)
            def _():
                copy = pltpu.make_async_copy(
                    packed.at[pl.ds(d * stride + capacity, over.shape[1])],
                    over.at[lax.rem(here[0] + d, devices)],
                    sems.at[1, d],
                )
                copy.start()
                copy.wait()


def send_rows(capacity, beyond, devices, here, shift_rows, q, state, eddy, halos):
    levels, rows = q.shape[:2]
    chunk = 16
    return pl.pallas_call(
        functools.partial(send_rows_kernel, chunk),
        grid=(levels // chunk,),
        in_specs=[
            SCALARS,
            SCALARS,
            WHOLE,
            pl.BlockSpec((3, chunk, rows, LANES), lambda i: (0, i, 0, 0)),
            pl.BlockSpec((chunk, rows, LANES), lambda i: (i, 0, 0)),
        ]
        + [WHOLE] * 4,
        out_specs=[ANYWHERE] * 2,
        out_shape=[
            f32((devices, capacity, LANES)),
            f32((devices, beyond, LANES)),
        ],
        scratch_shapes=[
            pltpu.VMEM((devices * (capacity + beyond + rows), LANES), jnp.float32),
            pltpu.VMEM((UNROLL, rows + 16, LANES), jnp.float32),
            pltpu.VMEM((UNROLL, 2 * rows, LANES), jnp.float32),
            pltpu.SMEM((devices,), jnp.int32),
            pltpu.SemaphoreType.DMA((2, devices)),
        ],
        compiler_params=params(63),
        name="send_rows",
    )(here, shift_rows, q, state, eddy, *halos)


def place_rows_kernel(here, sent, shift_rows, starts, screen_of_level, got, over, out, extra, held, tiles, filled, sems):
    devices, capacity = got.shape[:2]
    owners, slots, rows = out.shape[:3]
    levels = shift_rows.shape[0]
    stride = capacity + over.shape[1]
    per_owner = NS // owners
    me = here[0]
    copies = [
        pltpu.make_async_copy(got.at[d], held.at[pl.ds(rows + d * stride, capacity)], sems.at[0, d])
        for d in range(devices)
    ]
    for copy in copies:
        copy.start()
    for d in range(devices):
        filled[d] = 0
    for copy in copies:
        copy.wait()
    for d in range(devices):

        @pl.when(sent[lax.rem(me - d + devices, devices)] > capacity)
        def _():
            copy = pltpu.make_async_copy(
                over.at[d], held.at[pl.ds(rows + d * stride + capacity, over.shape[1])], sems.at[1, d]
            )
            copy.start()
            copy.wait()

    row = lax.broadcasted_iota(jnp.int32, (rows, LANES), 0)

    def place(level, carry):
        block, after, rest, near, far = row_places(shift_rows, filled, level, rows, devices)
        near_from = lax.select(me >= block, me - block, me - block + devices)
        far_from = lax.select(me >= after, me - after, me - after + devices)
        near_tile = held[pl.ds(rows + near_from * stride + near - rest, rows), :]
        far_tile = held[pl.ds(rows + far_from * stride + far, rows), :]
        owner = lax.div(screen_of_level[level], per_owner)
        tiles[owner, level - starts[owner]] = jnp.where(row < rest, far_tile, near_tile)
        return carry

    half = owners // 2
    middle = starts[half]
    pairs = lax.div(middle, 2)
    lax.fori_loop(0, pairs, lambda i, c: place(2 * i + 1, place(2 * i, c)), 0)
    lax.fori_loop(2 * pairs, middle, place, 0)
    copies = [
        pltpu.make_async_copy(tiles.at[at, pl.ds(0, slots)], out.at[at], sems.at[0, n])
        for n, at in enumerate((pl.ds(0, half), pl.ds(half, half)))
    ]
    copies[0].start()
    pairs = lax.div(levels - middle, 2)
    lax.fori_loop(0, pairs, lambda i, c: place(middle + 2 * i + 1, place(middle + 2 * i, c)), 0)
    lax.fori_loop(middle + 2 * pairs, levels, place, 0)
    copies[1].start()
    most = starts[1]
    for g in range(1, owners):
        most = jnp.maximum(most, starts[g + 1] - starts[g])

    @pl.when(most > slots)
    def _():
        copy = pltpu.make_async_copy(tiles.at[:, pl.ds(slots, extra.shape[1])], extra, sems.at[1, 0])
        copy.start()
        copy.wait()

    for copy in copies:
        copy.wait()


def place_rows(here, sent, shift_rows, starts, screen_of_level, got, over, owners, rows, slots, most):
    devices = got.shape[0]
    levels = shift_rows.shape[0]
    return pl.pallas_call(
        place_rows_kernel,
        in_specs=[SCALARS] * 5 + [ANYWHERE] * 2,
        out_specs=[ANYWHERE] * 2,
        out_shape=[f32((owners, slots, rows, LANES)), f32((owners, most - slots, rows, LANES))],
        scratch_shapes=[
            pltpu.VMEM((devices * (got.shape[1] + over.shape[1]) + 2 * rows, LANES), jnp.float32),
            pltpu.VMEM((owners, most, rows, LANES), jnp.float32),
            pltpu.SMEM((devices,), jnp.int32),
            pltpu.SemaphoreType.DMA((2, devices)),
        ],
        compiler_params=params(63),
        name="place_rows",
    )(here, sent, shift_rows, starts, screen_of_level, got, over)


def sum_screens_kernel(here, starts, shift_cols, screen_of_level, got, extra, out):
    owners, slots = got.shape[:2]
    screens, rows = out.shape[:2]
    me = here[1]
    first = starts[me]
    lane = lax.broadcasted_iota(jnp.int32, (rows, LANES), 1)
    out[...] = jnp.zeros(out.shape, jnp.float32)

    def add(source, index, at):
        level = first + index
        shift = shift_cols[level]
        block, rest = shift // LANES, lax.rem(shift, LANES)
        screen = screen_of_level[level] - me * screens
        for t in range(owners):
            near = source[lax.rem(t - block + owners, owners), at]
            far = source[lax.rem(t - block - 1 + owners, owners), at]
            both = pltpu.roll(jnp.where(lane < LANES - rest, near, far), rest, 1)
            out[screen, :, t * LANES : (t + 1) * LANES] += both

    count = starts[me + 1] - first

    def body(index, carry):
        add(got, index, index)
        return carry

    def more(index, carry):
        add(extra, index, index - slots)
        return carry

    lax.fori_loop(0, jnp.minimum(count, slots), body, 0)
    lax.fori_loop(slots, jnp.maximum(count, slots), more, 0)


def sum_screens(here, starts, shift_cols, screen_of_level, got, extra, screens):
    owners, _, rows = got.shape[:3]
    return pl.pallas_call(
        sum_screens_kernel,
        in_specs=[SCALARS] * 4 + [WHOLE] * 2,
        out_specs=WHOLE,
        out_shape=f32((screens, rows, owners * LANES)),
        compiler_params=params(63),
        name="sum_screens",
    )(here, starts, shift_cols, screen_of_level, got, extra)


def swap(block, axis):
    return lax.all_to_all(block, axis, split_axis=0, concat_axis=0, tiled=True)


ROWS_AT_ONCE = 256
ROWS_MORE = 48
LEVELS_AT_ONCE = 13


def swap_more(over, first, need):
    part = ROWS_MORE
    rounds = jnp.maximum(need - first + part - 1, 0) // part

    def body(carry):
        done, over = carry
        piece = lax.dynamic_slice_in_dim(over, done * part, part, 1)
        return done + 1, lax.dynamic_update_slice_in_dim(over, swap(piece, "gx"), done * part, 1)

    return lax.while_loop(lambda carry: carry[0] < rounds, body, (jnp.int32(0), over))[1]


def swap_extra(extra, needed):
    body = lambda carry: (carry[0] - 1, swap(carry[1], "gy"))
    return lax.while_loop(lambda carry: carry[0] > 0, body, (needed.astype(jnp.int32), extra))[1]


def local(state, eddy, shift_rows, shift_cols, screen_of_level):
    levels, rows = state.shape[1:3]
    devices, owners = lax.axis_size("gx"), lax.axis_size("gy")
    per_owner = NS // owners
    most = 4 * per_owner
    here = jnp.stack([lax.axis_index("gx"), lax.axis_index("gy")]).astype(jnp.int32)

    block, rest = shift_rows // rows, shift_rows % rows
    place = jnp.arange(devices, dtype=jnp.int32)[:, None]
    rows_sent = jnp.sum(
        jnp.where(place == block[None], rows - rest[None], 0)
        + jnp.where(place == (block[None] + 1) % devices, rest[None], 0),
        axis=1,
    )
    bounds = per_owner * jnp.arange(owners + 1, dtype=jnp.int32)[:, None]
    starts = jnp.sum((screen_of_level[None] < bounds).astype(jnp.int32), axis=1)
    most_rows = jnp.max(rows_sent)
    most_levels = jnp.max(starts[1:] - starts[:-1])

    q, *edges = q_edges(state)
    q_halos = exchange(edges)

    beyond = -(-(levels * rows - ROWS_AT_ONCE) // ROWS_MORE) * ROWS_MORE
    out, over = send_rows(ROWS_AT_ONCE, beyond, devices, here, shift_rows, q, state, eddy, q_halos)
    got = swap(out, "gx")
    halos = exchange(state_edges(state, out))
    over = swap_more(over, ROWS_AT_ONCE, most_rows)
    out, extra = place_rows(
        here, rows_sent, shift_rows, starts, screen_of_level, got, over, owners, rows, LEVELS_AT_ONCE, most
    )
    out, extra, *halos = lax.optimization_barrier((out, extra, *halos))
    got = swap(out, "gy")
    advanced = advance(state, eddy, halos, q_halos, out)
    extra = swap_extra(extra, most_levels > LEVELS_AT_ONCE)
    screens = sum_screens(here, starts, shift_cols, screen_of_level, got, extra, per_owner)
    return advanced, screens


def solution(mesh):
    placed = (P(None, None, "gx", "gy"), P(None, "gx", "gy"), P(), P(), P())
    return jax.shard_map(
        local,
        mesh=mesh,
        in_specs=placed,
        out_specs=(P(None, None, "gx", "gy"), P("gy", "gx", None)),
        check_vma=False,
    )
```
